512 devices in a mesh: dom: 128 (over z_lo, x, y, core), rep: 4 (over z_hi).
Axes of the slice: x: 4, y: 4, z: 16 (z_hi: 4, z_lo: 4; z = z_hi * 4 + z_lo), core: 2. Of those that a mesh axis runs over, the one named last changes fastest.
Arguments:
- feat: bfloat16 [4, 8192, 128], P('rep', 'dom'), may hold values from -6 to 6
- species: int32 [4, 8192], P('rep', 'dom'), may hold values from 0 to 4
- species_gain: float32 [5, 128], replicated, may hold values from 0.5 to 2
- send_lists: int32 [4, 6, 3072], P('rep', None, 'dom'), may hold values from 0 to 63
- edge_src: int32 [4, 524288], P('rep', 'dom'), may hold values from 0 to 207
- edge_dst: int32 [4, 524288], P('rep', 'dom'), may hold values from 0 to 63
- edge_vec: float32 [4, 3, 524288], P('rep', None, 'dom'), may hold values from -3.4 to 3.4
- w_rad: float32 [8, 128], replicated, may hold values from -2 to 2
- w_mix: bfloat16 [384, 128], replicated, may hold values from -0.3125 to 0.3125
- out_cot: bfloat16 [4, 8192, 128], P('rep', 'dom'), may hold values from -6 to 6
Outputs:
- d_feat: float32 [4, 8192, 128], P('rep', 'dom')
- grad_mix: float32 [384, 128], replicated
- grad_rad: float32 [8, 128], replicated
The draws below stay inside these ranges and needn't reach their ends.
Inputs may be any that keep to these rules, and one draw needn't show every extreme that they name: `send_lists`: own rows of the sending domain. `edge_src`: rows below 64 are owned atoms; then come six blocks of 24 rows, block g from the domain across face g. `edge_dst`: owned rows of the domain.
All inputs are finite; a program needn't handle non-finite values.
Results may differ from the reference program's by a relative error of at most 0.012.
The reference program's roundings to bfloat16 on the way count: a program that leaves them out, or rounds other values in their place, can miss the bound.
Values may be sent and summed in bfloat16 or wider, within the bound.
No kernel may reach another device: no remote copies, remote signals or barrier semaphores. Data moves between devices by JAX's collectives and lax.ppermute only.
A program may use at most 64 MiB of HBM per device.

```python
import math
import jax
import jax.numpy as jnp
from jax import lax

C = 128
NB = 8
NSPEC = 5
A_DEV = 64
GHOST = 24
E_DEV = 4096
NZ_DOM = 8
NY_DOM = 4
ATOMS = 8192
EDGES = 524288
SENDS = 3072
REPS = 4
N_DOM = 128
N_REP = 4


def with_ends(array, key, smallest, top_value):
    index_at = [jax.random.randint(jax.random.fold_in(key, axis), (), 0, length) for axis, length in enumerate(array.shape)]
    main_axis = array.shape.index(max(array.shape))
    next_to = index_at[:main_axis] + [(index_at[main_axis] + 1) % array.shape[main_axis]] + index_at[main_axis + 1:]
    return array.at[tuple(index_at)].set(smallest).at[tuple(next_to)].set(top_value)


def levels(key, extent, pieces, smallest, largest):
    level = 1.0
    for position, blocks in pieces:
        steps = jax.random.uniform(jax.random.fold_in(jax.random.fold_in(key, 6), position), (blocks,), jnp.float32, smallest / len(pieces), largest / len(pieces))
        level = level * jnp.repeat(jnp.exp(steps), extent[position] // blocks).reshape((-1,) + (1,) * (len(extent) - 1 - position))
    return level


def bell_draw(stream_key, extent, spread, reach, cuts=(), kind=jnp.bfloat16):
    values = spread * jax.random.normal(stream_key, extent, jnp.float32)
    if cuts:
        values = values * levels(stream_key, extent, cuts, -0.22, 0.18)
    return jnp.clip(values, -reach, reach).astype(kind)


def setup_inputs(seed: int = 0) -> dict:
    splits = jax.random.split(jax.random.key(seed), 11)
    feat = bell_draw(splits[0], (REPS, ATOMS, C), 1.0, 6.0, ((0, 4), (1, 128)))
    species = with_ends(jax.random.randint(splits[1], (REPS, ATOMS), 0, NSPEC), jax.random.fold_in(splits[1], 1), 0, NSPEC - 1).astype(jnp.int32)
    species_gain = jnp.clip(jnp.exp(jax.random.uniform(splits[2], (NSPEC, C), jnp.float32, math.log(0.5), math.log(2.0))), 0.5, 2.0)
    send_lists = with_ends(jax.random.randint(splits[3], (REPS, 6, SENDS), 0, A_DEV), jax.random.fold_in(splits[3], 1), 0, A_DEV - 1).astype(jnp.int32)
    edge_src = with_ends(jax.random.randint(splits[4], (REPS, EDGES), 0, A_DEV + 6 * GHOST), jax.random.fold_in(splits[4], 1), 0, (A_DEV + 6 * GHOST) - 1).astype(jnp.int32)
    edge_dst = with_ends(jax.random.randint(splits[5], (REPS, EDGES), 0, A_DEV), jax.random.fold_in(splits[5], 1), 0, A_DEV - 1).astype(jnp.int32)
    edge_vec = jnp.clip(jax.random.uniform(splits[6], (REPS, 3, EDGES), jnp.float32, -3.4, 3.4) * levels(splits[6], (REPS, 3, EDGES), ((0, 4), (2, 128)), -0.4, 0.0), -3.4, 3.4)
    w_rad = bell_draw(splits[7], (NB, C), NB ** -0.5, 2.0, (), jnp.float32)
    w_mix = bell_draw(splits[8], (3 * C, C), (3 * C) ** -0.5, 0.3125)
    out_cot = bell_draw(splits[9], (REPS, ATOMS, C), 1.0, 6.0, ((0, 4), (1, 128)))
    return dict(feat=feat, species=species, species_gain=species_gain, send_lists=send_lists, edge_src=edge_src, edge_dst=edge_dst, edge_vec=edge_vec, w_rad=w_rad, w_mix=w_mix, out_cot=out_cot)


msg_scale = 0.35
cutoff = 6.0
clip_norm = 256.0

def edge_geometry(vec, nbasis):
    radius = jnp.sqrt(vec[0] * vec[0] + vec[1] * vec[1] + vec[2] * vec[2] + 0.25)
    unit = vec / radius
    ux, uy, uz = (unit[0], unit[1], unit[2])
    root3 = jnp.sqrt(3.0)
    root5 = jnp.sqrt(5.0)
    root15 = jnp.sqrt(15.0)
    harm = jnp.stack([jnp.ones_like(ux), root3 * ux, root3 * uy, root3 * uz, root15 * ux * uy, root15 * uy * uz, 0.5 * root5 * (3.0 * uz * uz - 1.0), root15 * ux * uz, 0.5 * root15 * (ux * ux - uy * uy)])
    scaled = radius / cutoff
    envelope = (1.0 - scaled * scaled) ** 2
    orders = (jnp.arange(nbasis, dtype=jnp.int32) + 1).astype(jnp.float32)[:, None]
    basis = jnp.sin(orders * jnp.pi * radius[None, :] / cutoff) / radius[None, :] * envelope[None, :]
    return (harm, basis)

def edge_pass(rows, dst, vec, cot, w_rad, w_mix):
    atoms = cot.shape[0]
    chans = w_rad.shape[1]
    harm, basis = edge_geometry(vec, w_rad.shape[0])
    radial = lax.dot_general(basis, w_rad, (((0,), (0,)), ((), ())), precision=lax.Precision.HIGHEST)
    source = rows.astype(jnp.float32)
    message = radial * source
    moments = [msg_scale * jax.ops.segment_sum(harm[k][:, None] * message, dst, num_segments=atoms) for k in range(9)]
    group_zero = moments[0] * moments[0]
    group_one = moments[1] * moments[1] + moments[2] * moments[2] + moments[3] * moments[3]
    group_two = moments[4] * moments[4]
    for k in range(5, 9):
        group_two = group_two + moments[k] * moments[k]
    invariants = jnp.concatenate([group_zero, group_one, group_two], axis=1).astype(jnp.bfloat16)
    pre = jnp.dot(invariants, w_mix, preferred_element_type=jnp.float32)
    sigma = jax.nn.sigmoid(pre)
    slope = sigma * (1.0 + pre * (1.0 - sigma))
    dpre = (cot.astype(jnp.float32) * slope).astype(jnp.bfloat16)
    gmix = lax.dot_general(invariants, dpre, (((0,), (0,)), ((), ())), preferred_element_type=jnp.float32)
    dinv = lax.dot_general(dpre, w_mix, (((1,), (1,)), ((), ())), preferred_element_type=jnp.float32)
    groups = [0, 1, 1, 1, 2, 2, 2, 2, 2]
    dmessage = jnp.zeros_like(message)
    for k in range(9):
        start = groups[k] * chans
        dmoment = 2.0 * moments[k] * dinv[:, start:start + chans]
        dmessage = dmessage + harm[k][:, None] * dmoment[dst]
    dmessage = msg_scale * dmessage
    dradial = dmessage * source
    dsource = dmessage * radial
    grad_r = lax.dot_general(basis, dradial, (((1,), (0,)), ((), ())), precision=lax.Precision.HIGHEST)
    return (dsource, gmix, grad_r)

def add_rows(base, index, values):
    return base.at[index].add(values)

def reference(feat, species, species_gain, send_lists, edge_src, edge_dst, edge_vec, w_rad, w_mix, out_cot):
    onehot = (species[..., None] == jnp.arange(NSPEC, dtype=jnp.int32)).astype(jnp.float32)
    gain = jnp.einsum('rak,kc->rac', onehot, species_gain, precision=lax.Precision.HIGHEST)
    own = (feat.astype(jnp.float32) * gain).astype(jnp.bfloat16).reshape(N_REP, N_DOM, A_DEV, C)
    lists = send_lists.reshape(N_REP, 6, N_DOM, GHOST)
    offsets = [1, -1, NZ_DOM, -NZ_DOM, NZ_DOM * NY_DOM, -NZ_DOM * NY_DOM]
    blocks = [own]
    for face in range(6):
        sent = jnp.take_along_axis(own, lists[:, face, :, :, None], axis=2)
        blocks.append(jnp.roll(sent, offsets[face], axis=1))
    extended = jnp.concatenate(blocks, axis=2)
    width = A_DEV + 6 * GHOST
    extended = extended.reshape(N_REP * N_DOM, width, C)
    sources = edge_src.reshape(N_REP * N_DOM, E_DEV)
    targets = edge_dst.reshape(N_REP * N_DOM, E_DEV)
    vectors = edge_vec.reshape(N_REP, 3, N_DOM, E_DEV).transpose(0, 2, 1, 3).reshape(N_REP * N_DOM, 3, E_DEV)
    cots = out_cot.reshape(N_REP * N_DOM, A_DEV, C)

    def one_domain(items):
        ext_rows, src, dst, vec, cot = items
        dsource, gmix, grad_r = edge_pass(ext_rows[src], dst, vec, cot, w_rad, w_mix)
        return (jax.ops.segment_sum(dsource, src, num_segments=width), gmix, grad_r)
    dext, gmix_all, grad_all = lax.map(one_domain, (extended, sources, targets, vectors, cots))
    gmix = lax.optimization_barrier(jnp.sum(gmix_all, axis=0))
    grad_r = lax.optimization_barrier(jnp.sum(grad_all, axis=0))
    dext = dext.reshape(N_REP, N_DOM, width, C)
    adder = jax.vmap(jax.vmap(add_rows))
    total = dext[:, :, :A_DEV]
    for face in range(6):
        start = A_DEV + face * GHOST
        returned = jnp.roll(dext[:, :, start:start + GHOST], -offsets[face], axis=1)
        total = adder(total, lists[:, face], returned)
    d_feat = total.reshape(N_REP, ATOMS, C) * gain
    norm = jnp.sqrt(jnp.sum(gmix * gmix) + jnp.sum(grad_r * grad_r))
    factor = clip_norm / jnp.maximum(norm, clip_norm)
    return (d_feat, factor * gmix, factor * grad_r)
```

```python
import jax
import jax.numpy as jnp
import numpy as np
from jax import lax
from jax.experimental import pallas as pl
from jax.experimental.pallas import tpu as pltpu
from jax.sharding import Mesh, PartitionSpec as P

msg_scale = 0.35
cutoff = 6.0
clip_norm = 256.0
f32, bf16 = jnp.float32, jnp.bfloat16

CHANS = 128
NB = 8
ATOMS = 64
FACES = 6
PAD = 32
GHOST = 24
ROWS = ATOMS + FACES * PAD
EDGES = 4096
CHUNK = 1024
GROUP = 32
SLOT = 16
SLAB = ("x", "y", "core")
LINE = ("zl", "rep")
DOM = ("zl", "x", "y", "core")
STEPS = (1, 8, 32)
HIGH = lax.Precision.HIGHEST
VMEM_LIMIT = 48 * 1024 * 1024


def dot(a, b, dims, precision=None):
    return lax.dot_general(
        a, b, (dims, ((), ())), precision=precision, preferred_element_type=f32
    )


def rows_iota(shape):
    return lax.broadcasted_iota(jnp.int32, shape, 0)


def call(kernel, outs, *args, scratch=(), cost=None):
    def spec(a):
        return pl.BlockSpec(memory_space=pltpu.VMEM)

    return pl.pallas_call(
        kernel,
        out_shape=outs,
        in_specs=[spec(a) for a in args],
        out_specs=[spec(o) for o in outs],
        scratch_shapes=list(scratch),
        cost_estimate=cost,
        compiler_params=pltpu.CompilerParams(vmem_limit_bytes=VMEM_LIMIT),
    )(*args)


def pre_kernel(feat_ref, species_ref, gain_ref, sends_ref, own_ref, gain_out, pick_ref):
    hot = (rows_iota((8, ATOMS)) == species_ref[...]).astype(f32)
    gains = jnp.concatenate([gain_ref[...], jnp.zeros((3, CHANS), f32)], axis=0)
    gain = dot(hot, gains, ((0,), (0,)), HIGH)
    own = (feat_ref[0].astype(f32) * gain).astype(bf16)
    own_ref[...] = own
    gain_out[...] = gain
    dom = domain()
    for face in range(FACES):
        hot = (rows_iota((ATOMS, GHOST)) == sends_ref[0, face : face + 1, :]).astype(f32)
        hot = jnp.concatenate([hot, jnp.zeros((ATOMS, PAD - GHOST), f32)], axis=1)
        picked = dot(hot.astype(bf16), own, ((0,), (0,)))
        bit = lax.rem(dom // STEPS[face // 2], 2)
        pick_ref[2 * (face // 2) + lax.rem(bit + face % 2, 2)] = picked.astype(bf16)


def domain():
    z, x, y, c = (lax.axis_index(a) for a in DOM)
    return ((z * 4 + x) * 4 + y) * 2 + c


def geo_kernel(vec_ref, harm_ref, basis_ref):
    vx, vy, vz = (vec_ref[0, i : i + 1, :] for i in range(3))
    square = vx * vx + vy * vy + vz * vz + 0.25
    inv_r = lax.rsqrt(square)
    radius = square * inv_r
    ux, uy, uz = vx * inv_r, vy * inv_r, vz * inv_r
    r3, r5, r15 = 3.0**0.5, 5.0**0.5, 15.0**0.5
    harms = [
        jnp.ones_like(ux),
        r3 * ux,
        r3 * uy,
        r3 * uz,
        r15 * ux * uy,
        r15 * uy * uz,
        0.5 * r5 * (3.0 * uz * uz - 1.0),
        r15 * ux * uz,
        0.5 * r15 * (ux * ux - uy * uy),
    ]
    for k, h in enumerate(harms):
        harm_ref[k : k + 1, :] = h
    scaled = radius * (1.0 / cutoff)
    envelope = 1.0 - scaled * scaled
    envelope = envelope * envelope * inv_r
    t = scaled * np.float32(np.pi) - np.float32(np.pi / 2)
    t2 = t * t
    sin_t = series(t2, 1) * t
    cos_t = series(t2, 0)
    twice = -2.0 * sin_t
    before, now = jnp.zeros_like(t), cos_t * envelope
    for b in range(NB):
        basis_ref[b : b + 1, :] = now
        before, now = now, twice * now - before


def series(square, odd):
    terms = [(-1.0) ** n / float(np.prod(np.arange(1, 2 * n + odd + 1.0))) for n in range(9)]
    total = jnp.full_like(square, terms[-1])
    for term in terms[-2::-1]:
        total = total * square + term
    return total


def split(values):
    top = values.astype(bf16).astype(f32)
    return top, values - top


def main_kernel(
    own_ref, r0, r1, r2, r3, r4, r5, src_ref, dst_ref, harm_ref, basis_ref, wrad_ref, wmix_ref, cot_ref,
    dext_ref, back_ref, grad_ref,
    hot_s, harm_s, radial_s, source_s, mom_s, dmom_s,
):
    dom = domain()
    got = (r0, r1, r2, r3, r4, r5)
    blocks = [own_ref[...].astype(f32)]
    bits = [lax.rem(dom // step, 2) for step in STEPS]
    for face in range(FACES):
        pair = face // 2
        a, b = got[2 * pair][...].astype(f32), got[2 * pair + 1][...].astype(f32)
        swapped = lax.rem(bits[pair] + face % 2, 2) == 0
        blocks.append(jnp.where(swapped, b, a))
    ext = jnp.concatenate(blocks, axis=0).T.astype(bf16)
    w_top, w_low = split(wrad_ref[...])
    wrad = jnp.concatenate([w_top, w_low, w_top], axis=0).T.astype(bf16)
    mom_s[...] = jnp.zeros_like(mom_s)
    for start in range(0, EDGES, CHUNK):
        at = pl.ds(start, CHUNK)
        src = src_ref[:, at]
        shift = jnp.zeros_like(src)
        for face in range(1, FACES):
            shift = shift + jnp.where(src >= ATOMS + face * GHOST, PAD - GHOST, 0)
        hot = jnp.where(rows_iota((ROWS, CHUNK)) == src + shift, 1.0, 0.0).astype(bf16)
        hot_s[:, at] = hot
        source = dot(ext, hot, ((1,), (0,)))
        source_s[:, at] = source.astype(bf16)
        b_top, b_low = split(basis_ref[:, at])
        basis = jnp.concatenate([b_top, b_top, b_low], axis=0).astype(bf16)
        radial = dot(wrad, basis, ((1,), (0,)))
        radial_s[:, at] = radial
        message = (radial * source).astype(bf16)
        own_hot = rows_iota((ATOMS, CHUNK)) == dst_ref[:, at]
        harm_s[0:ATOMS, at] = jnp.where(own_hot, 1.0, 0.0).astype(bf16)
        for k in range(1, 9):
            harm = harm_ref[k : k + 1, at]
            harm_s[k * ATOMS : (k + 1) * ATOMS, at] = jnp.where(own_hot, harm, 0.0).astype(bf16)
        mom_s[...] += dot(harm_s[:, at], message, ((1,), (1,)))
    moments = [msg_scale * mom_s[k * ATOMS : (k + 1) * ATOMS, :] for k in range(9)]
    squares = [m * m for m in moments]
    two = squares[4]
    for k in range(5, 9):
        two = two + squares[k]
    inv = jnp.concatenate([squares[0], squares[1] + squares[2] + squares[3], two], axis=1).astype(bf16)
    pre = dot(inv, wmix_ref[...], ((1,), (0,)))
    sigma = jax.nn.sigmoid(pre)
    slope = sigma * (1.0 + pre * (1.0 - sigma))
    dpre = (cot_ref[0].astype(f32) * slope).astype(bf16)
    grad_ref[0 : 3 * CHANS, :] = dot(inv, dpre, ((0,), (0,))).astype(bf16)
    dinv = dot(dpre, wmix_ref[...], ((1,), (1,)))
    groups = [0, 1, 1, 1, 2, 2, 2, 2, 2]
    for k in range(9):
        part = dinv[:, groups[k] * CHANS : (groups[k] + 1) * CHANS]
        mom_s[k * ATOMS : (k + 1) * ATOMS, :] = (2.0 * msg_scale) * moments[k] * part
    dmom_s[...] = mom_s[...].T.astype(bf16)
    dext = jnp.zeros((ROWS, CHANS), f32)
    gradr = jnp.zeros((2 * NB, CHANS), f32)
    for start in range(0, EDGES, CHUNK):
        at = pl.ds(start, CHUNK)
        dmsg = dot(dmom_s[...], harm_s[:, at], ((1,), (0,)))
        dradial = dmsg * source_s[:, at].astype(f32)
        dsource = (dmsg * radial_s[:, at]).astype(bf16)
        dext = dext + dot(hot_s[:, at], dsource, ((1,), (1,)))
        b_top, b_low = split(basis_ref[:, at])
        basis = jnp.concatenate([b_top, b_low], axis=0).astype(bf16)
        gradr = gradr + dot(basis, dradial.astype(bf16), ((1,), (1,)))
    gradr = jnp.concatenate([gradr[:NB] + gradr[NB:], jnp.zeros((NB, CHANS), f32)], axis=0)
    grad_ref[3 * CHANS : 3 * CHANS + 2 * NB, :] = gradr.astype(bf16)
    rest = GROUP * SLOT - 3 * CHANS - 2 * NB
    grad_ref[3 * CHANS + 2 * NB :, :] = jnp.zeros((rest, CHANS), bf16)
    dext_ref[...] = dext[:ATOMS]
    for face in range(FACES):
        pair = face // 2
        start = ATOMS + face * PAD
        slot = 2 * pair + lax.rem(bits[pair] + face % 2 + 1, 2)
        back_ref[slot] = dext[start : start + PAD].astype(bf16)


def post_kernel(dext_ref, gain_ref, sends_ref, r0, r1, r2, r3, r4, r5, sums_ref, dfeat_ref, gmix_ref, grad_ref):
    dom = domain()
    got = (r0, r1, r2, r3, r4, r5)
    total = dext_ref[...]
    for face in range(FACES):
        pair = face // 2
        bit = lax.rem(dom // STEPS[pair], 2)
        a, b = got[2 * pair][...].astype(f32), got[2 * pair + 1][...].astype(f32)
        values = jnp.where(lax.rem(bit + face % 2, 2) == 0, a, b)[:GHOST].astype(bf16)
        hot = (rows_iota((ATOMS, GHOST)) == sends_ref[0, face : face + 1, :]).astype(f32)
        total = total + dot(hot.astype(bf16), values, ((1,), (0,)))
    dfeat_ref[0] = total * gain_ref[...]
    sums = sums_ref[0 : 3 * CHANS + 2 * NB, :].astype(f32)
    gmix, grad = sums[: 3 * CHANS], sums[3 * CHANS : 3 * CHANS + NB]
    norm = jnp.sqrt(jnp.sum(gmix * gmix, keepdims=True) + jnp.sum(grad * grad, keepdims=True))
    factor = clip_norm / jnp.maximum(norm, clip_norm)
    gmix_ref[...] = factor * gmix
    grad_ref[...] = factor * grad


def swap(block, step, parity):
    pairs = []
    for i in range(128):
        if (i // step) % 2 == parity:
            j = (i + step) % 128
            pairs += [(i, j), (j, i)]
    return lax.ppermute(block, DOM, pairs)


def reduce_all(grads):
    parts = lax.all_to_all(grads, SLAB, 0, 0, tiled=True)
    mine = parts.reshape(GROUP, SLOT, CHANS).astype(f32).sum(0).astype(bf16)
    parts = lax.all_to_all(jnp.tile(mine, (16, 1)), LINE, 0, 0, tiled=True)
    mine = parts.reshape(16, SLOT, CHANS).astype(f32).sum(0).astype(bf16)
    return lax.all_to_all(jnp.tile(mine, (GROUP, 1)), SLAB, 0, 0, tiled=True)


def on_device(feat, species, species_gain, send_lists, edge_src, edge_dst, edge_vec, w_rad, w_mix, out_cot):
    shape = jax.ShapeDtypeStruct
    own, gain, picks = call(
        pre_kernel,
        [shape((ATOMS, CHANS), bf16), shape((ATOMS, CHANS), f32), shape((FACES, PAD, CHANS), bf16)],
        feat, species, species_gain, send_lists,
    )
    got = [swap(picks[2 * p + q], STEPS[p], q) for p in range(3) for q in range(2)]
    harm, basis = call(
        geo_kernel,
        [shape((16, EDGES), f32), shape((NB, EDGES), f32)],
        edge_vec,
        cost=pl.CostEstimate(flops=1000000, bytes_accessed=400000, transcendentals=0),
    )
    dext, back, grads = call(
        main_kernel,
        [shape((ATOMS, CHANS), f32), shape((FACES, PAD, CHANS), bf16), shape((GROUP * SLOT, CHANS), bf16)],
        own, *got, edge_src, edge_dst, harm, basis, w_rad, w_mix, out_cot,
        scratch=[
            pltpu.VMEM((ROWS, EDGES), bf16),
            pltpu.VMEM((9 * ATOMS, EDGES), bf16),
            pltpu.VMEM((CHANS, EDGES), f32),
            pltpu.VMEM((CHANS, EDGES), bf16),
            pltpu.VMEM((9 * ATOMS, CHANS), f32),
            pltpu.VMEM((CHANS, 9 * ATOMS), bf16),
        ],
    )
    returned = [swap(back[2 * p + q], STEPS[p], q) for p in range(3) for q in range(2)]
    sums = reduce_all(grads)
    d_feat, gmix, grad_r = call(
        post_kernel,
        [shape((1, ATOMS, CHANS), f32), shape((3 * CHANS, CHANS), f32), shape((NB, CHANS), f32)],
        dext, gain, send_lists, *returned, sums,
    )
    return d_feat, gmix, grad_r


def solution(mesh):
    fine = Mesh(mesh.devices.reshape(4, 4, 4, 2, 4), DOM + ("rep",))
    in_specs = (
        P("rep", DOM, None),
        P("rep", DOM),
        P(),
        P("rep", None, DOM),
        P("rep", DOM),
        P("rep", DOM),
        P("rep", None, DOM),
        P(),
        P(),
        P("rep", DOM, None),
    )
    out_specs = (P("rep", DOM, None), P(), P())
    return jax.shard_map(
        on_device, mesh=fine, in_specs=in_specs, out_specs=out_specs, check_vma=False
    )
```

```python
import jax
import jax.numpy as jnp
import numpy as np
from jax import lax
from jax.experimental import pallas as pl
from jax.experimental.pallas import tpu as pltpu
from jax.sharding import Mesh, PartitionSpec as P

msg_scale = 0.35
cutoff = 6.0
clip_norm = 256.0
f32, bf16 = jnp.float32, jnp.bfloat16

CHANS = 128
NB = 8
ATOMS = 64
FACES = 6
PAD = 32
GHOST = 24
ROWS = ATOMS + FACES * PAD
EDGES = 4096
CHUNK = 1024
SHARD = 32
BLOCKS = 16
PLANE = ("zl", "x")
REST = ("y", "core", "rep")
PEERS = 32
DOM = ("zl", "x", "y", "core")
STRIDES = (1, -1, 4, -4)
HIGH = lax.Precision.HIGHEST
VMEM_LIMIT = 48 * 1024 * 1024


def dot(a, b, dims, precision=None):
    return lax.dot_general(
        a, b, (dims, ((), ())), precision=precision, preferred_element_type=f32
    )


def rows_iota(shape):
    return lax.broadcasted_iota(jnp.int32, shape, 0)


def call(kernel, outs, *args, scratch=(), cost=None):
    def spec(a):
        return pl.BlockSpec(memory_space=pltpu.VMEM)

    return pl.pallas_call(
        kernel,
        out_shape=outs,
        in_specs=[spec(a) for a in args],
        out_specs=[spec(o) for o in outs],
        scratch_shapes=list(scratch),
        cost_estimate=cost,
        compiler_params=pltpu.CompilerParams(vmem_limit_bytes=VMEM_LIMIT),
    )(*args)


def pre_kernel(feat_ref, species_ref, gain_ref, sends_ref, own_ref, gain_out, pair_ref, pick_ref):
    hot = (rows_iota((8, ATOMS)) == species_ref[...]).astype(f32)
    gains = jnp.concatenate([gain_ref[...], jnp.zeros((3, CHANS), f32)], axis=0)
    gain = dot(hot, gains, ((0,), (0,)), HIGH)
    own = (feat_ref[0].astype(f32) * gain).astype(bf16)
    own_ref[...] = own
    gain_out[...] = gain
    plane, bit = position()
    pick_ref[...] = jnp.zeros_like(pick_ref)
    for face in range(FACES):
        hot = (rows_iota((ATOMS, GHOST)) == sends_ref[face]).astype(f32)
        hot = jnp.concatenate([hot, jnp.zeros((ATOMS, PAD - GHOST), f32)], axis=1)
        picked = dot(hot.astype(bf16), own, ((0,), (0,))).astype(bf16)
        if face < 2:
            pair_ref[lax.rem(bit + face, 2)] = picked
        else:
            pick_ref[lax.rem(plane + STRIDES[face - 2] + BLOCKS, BLOCKS)] = picked


def position():
    return lax.axis_index("zl") * 4 + lax.axis_index("x"), lax.axis_index("core")


def geo_kernel(vec_ref, harm_ref, basis_ref):
    vx, vy, vz = (vec_ref[i] for i in range(3))
    square = vx * vx + vy * vy + vz * vz + 0.25
    inv_r = lax.rsqrt(square)
    radius = square * inv_r
    ux, uy, uz = vx * inv_r, vy * inv_r, vz * inv_r
    r3, r5, r15 = 3.0**0.5, 5.0**0.5, 15.0**0.5
    harms = [
        jnp.ones_like(ux),
        r3 * ux,
        r3 * uy,
        r3 * uz,
        r15 * ux * uy,
        r15 * uy * uz,
        0.5 * r5 * (3.0 * uz * uz - 1.0),
        r15 * ux * uz,
        0.5 * r15 * (ux * ux - uy * uy),
    ]
    for k, h in enumerate(harms):
        harm_ref[k : k + 1, :] = h
    scaled = radius * (1.0 / cutoff)
    envelope = 1.0 - scaled * scaled
    envelope = envelope * envelope * inv_r
    t = scaled * np.float32(np.pi) - np.float32(np.pi / 2)
    t2 = t * t
    sin_t = series(t2, 1) * t
    cos_t = series(t2, 0)
    twice = -2.0 * sin_t
    before, now = jnp.zeros_like(t), cos_t * envelope
    for b in range(NB):
        basis_ref[b : b + 1, :] = now
        before, now = now, twice * now - before


def series(square, odd):
    terms = [(-1.0) ** n / float(np.prod(np.arange(1, 2 * n + odd + 1.0))) for n in range(9)]
    total = jnp.full_like(square, terms[-1])
    for term in terms[-2::-1]:
        total = total * square + term
    return total


def split(values):
    top = values.astype(bf16).astype(f32)
    return top, values - top


def main_kernel(
    own_ref, p0, p1, got_ref, src_ref, dst_ref, harm_ref, basis_ref, wrad_ref, wmix_ref, cot_ref,
    dext_ref, pair_ref, send_ref,
    hot_s, harm_s, radial_s, source_s, mom_s, dmom_s,
):
    plane, bit = position()
    a, b = p0[...].astype(f32), p1[...].astype(f32)
    blocks = [own_ref[...].astype(f32), jnp.where(bit == 0, b, a), jnp.where(bit == 0, a, b)]
    for stride in STRIDES:
        blocks.append(got_ref[lax.rem(plane - stride + BLOCKS, BLOCKS)].astype(f32))
    ext = jnp.concatenate(blocks, axis=0).T.astype(bf16)
    w_top, w_low = split(wrad_ref[...])
    wrad = jnp.concatenate([w_top, w_low, w_top], axis=0).T.astype(bf16)
    mom_s[...] = jnp.zeros_like(mom_s)
    for start in range(0, EDGES, CHUNK):
        at = pl.ds(start, CHUNK)
        src = src_ref[:, at]
        shift = jnp.zeros_like(src)
        for face in range(1, FACES):
            shift = shift + jnp.where(src >= ATOMS + face * GHOST, PAD - GHOST, 0)
        hot = jnp.where(rows_iota((ROWS, CHUNK)) == src + shift, 1.0, 0.0).astype(bf16)
        hot_s[:, at] = hot
        source = dot(ext, hot, ((1,), (0,)))
        source_s[:, at] = source.astype(bf16)
        b_top, b_low = split(basis_ref[:, at])
        basis = jnp.concatenate([b_top, b_top, b_low], axis=0).astype(bf16)
        radial = dot(wrad, basis, ((1,), (0,)))
        radial_s[:, at] = radial
        message = (radial * source).astype(bf16)
        own_hot = rows_iota((ATOMS, CHUNK)) == dst_ref[:, at]
        harm_s[0:ATOMS, at] = jnp.where(own_hot, 1.0, 0.0).astype(bf16)
        for k in range(1, 9):
            harm = harm_ref[k : k + 1, at]
            harm_s[k * ATOMS : (k + 1) * ATOMS, at] = jnp.where(own_hot, harm, 0.0).astype(bf16)
        mom_s[...] += dot(harm_s[:, at], message, ((1,), (1,)))
    moments = [msg_scale * mom_s[k * ATOMS : (k + 1) * ATOMS, :] for k in range(9)]
    squares = [m * m for m in moments]
    two = squares[4]
    for k in range(5, 9):
        two = two + squares[k]
    inv = jnp.concatenate([squares[0], squares[1] + squares[2] + squares[3], two], axis=1).astype(bf16)
    pre = dot(inv, wmix_ref[...], ((1,), (0,)))
    sigma = jax.nn.sigmoid(pre)
    slope = sigma * (1.0 + pre * (1.0 - sigma))
    dpre = (cot_ref[0].astype(f32) * slope).astype(bf16)
    gmix = dot(inv, dpre, ((0,), (0,))).astype(bf16)
    for i in range(3 * CHANS // SHARD):
        send_ref[i, 0:SHARD] = gmix[i * SHARD : (i + 1) * SHARD]
    dinv = dot(dpre, wmix_ref[...], ((1,), (1,)))
    groups = [0, 1, 1, 1, 2, 2, 2, 2, 2]
    for k in range(9):
        part = dinv[:, groups[k] * CHANS : (groups[k] + 1) * CHANS]
        mom_s[k * ATOMS : (k + 1) * ATOMS, :] = (2.0 * msg_scale) * moments[k] * part
    dmom_s[...] = mom_s[...].T.astype(bf16)
    dext = jnp.zeros((ROWS, CHANS), f32)
    gradr = jnp.zeros((2 * NB, CHANS), f32)
    for start in range(0, EDGES, CHUNK):
        at = pl.ds(start, CHUNK)
        dmsg = dot(dmom_s[...], harm_s[:, at], ((1,), (0,)))
        dradial = dmsg * source_s[:, at].astype(f32)
        dsource = (dmsg * radial_s[:, at]).astype(bf16)
        dext = dext + dot(hot_s[:, at], dsource, ((1,), (1,)))
        b_top, b_low = split(basis_ref[:, at])
        basis = jnp.concatenate([b_top, b_low], axis=0).astype(bf16)
        gradr = gradr + dot(basis, dradial.astype(bf16), ((1,), (1,)))
    gradr = jnp.concatenate([gradr[:NB] + gradr[NB:], jnp.zeros((SHARD - NB, CHANS), f32)], axis=0)
    send_ref[3 * CHANS // SHARD, 0:SHARD] = gradr.astype(bf16)
    for i in range(3 * CHANS // SHARD + 1, BLOCKS):
        send_ref[i, 0:SHARD] = jnp.zeros((SHARD, CHANS), bf16)
    for i in range(BLOCKS):
        send_ref[i, SHARD:] = jnp.zeros((PAD, CHANS), bf16)
    dext_ref[...] = dext[:ATOMS]
    for face in range(FACES):
        start = ATOMS + face * PAD
        block = dext[start : start + PAD].astype(bf16)
        if face < 2:
            pair_ref[lax.rem(bit + face + 1, 2)] = block
        else:
            to = lax.rem(plane - STRIDES[face - 2] + BLOCKS, BLOCKS)
            send_ref[to, SHARD:] = block


def total_kernel(parts_ref, out_ref):
    total = parts_ref[0, :SHARD].astype(f32)
    for i in range(1, parts_ref.shape[0]):
        total = total + parts_ref[i, :SHARD].astype(f32)
    total = total.astype(bf16)
    for i in range(out_ref.shape[0]):
        out_ref[i] = total


def post_kernel(
    dext_ref, gain_ref, sends_ref, p0, p1, got_ref, sums_ref, dfeat_ref, gmix_ref, grad_ref
):
    plane, bit = position()
    a, b = p0[...].astype(f32), p1[...].astype(f32)
    blocks = [jnp.where(bit == 0, a, b), jnp.where(bit == 0, b, a)]
    for stride in STRIDES:
        blocks.append(got_ref[lax.rem(plane + stride + BLOCKS, BLOCKS), SHARD:].astype(f32))
    total = dext_ref[...]
    for face in range(FACES):
        hot = (rows_iota((ATOMS, GHOST)) == sends_ref[face]).astype(f32)
        values = blocks[face][:GHOST].astype(bf16)
        total = total + dot(hot.astype(bf16), values, ((1,), (0,)))
    dfeat_ref[0] = total * gain_ref[...]
    whole = 3 * CHANS // SHARD
    parts = [sums_ref[i].astype(f32) for i in range(whole)]
    grad = sums_ref[whole].astype(f32)[:NB]
    square = grad * grad
    for part in parts:
        for i in range(0, SHARD, NB):
            square = square + part[i : i + NB] * part[i : i + NB]
    norm = jnp.sqrt(jnp.sum(square, keepdims=True))
    factor = clip_norm / jnp.maximum(norm, clip_norm)
    for i, part in enumerate(parts):
        gmix_ref[i * SHARD : (i + 1) * SHARD, :] = factor * part
    grad_ref[...] = factor * grad


def swap(block, parity):
    pairs = []
    for i in range(parity, 128, 2):
        j = (i + 1) % 128
        pairs += [(i, j), (j, i)]
    return lax.ppermute(block, DOM, pairs)


def exchange(blocks, axes):
    return lax.all_to_all(blocks, axes, 0, 0, tiled=True)


def on_device(feat, species, species_gain, send_lists, edge_src, edge_dst, edge_vec, w_rad, w_mix, out_cot):
    shape = jax.ShapeDtypeStruct
    sends = send_lists.reshape(FACES, 1, GHOST)
    own, gain, pair, picks = call(
        pre_kernel,
        [
            shape((ATOMS, CHANS), bf16),
            shape((ATOMS, CHANS), f32),
            shape((2, PAD, CHANS), bf16),
            shape((BLOCKS, PAD, CHANS), bf16),
        ],
        feat, species, species_gain, sends,
    )
    near = [swap(pair[q], q) for q in range(2)]
    far = exchange(picks, PLANE)
    harm, basis = call(
        geo_kernel,
        [shape((16, EDGES), f32), shape((NB, EDGES), f32)],
        edge_vec.reshape(3, 1, EDGES),
        cost=pl.CostEstimate(flops=1000000, bytes_accessed=400000, transcendentals=0),
    )
    dext, pair, blocks = call(
        main_kernel,
        [
            shape((ATOMS, CHANS), f32),
            shape((2, PAD, CHANS), bf16),
            shape((BLOCKS, SHARD + PAD, CHANS), bf16),
        ],
        own, *near, far, edge_src, edge_dst, harm, basis, w_rad, w_mix, out_cot,
        scratch=[
            pltpu.VMEM((ROWS, EDGES), bf16),
            pltpu.VMEM((9 * ATOMS, EDGES), bf16),
            pltpu.VMEM((CHANS, EDGES), f32),
            pltpu.VMEM((CHANS, EDGES), bf16),
            pltpu.VMEM((9 * ATOMS, CHANS), f32),
            pltpu.VMEM((CHANS, 9 * ATOMS), bf16),
        ],
    )
    near = [swap(pair[q], q) for q in range(2)]
    far = exchange(blocks, PLANE)
    (parts,) = call(total_kernel, [shape((PEERS, SHARD, CHANS), bf16)], far)
    parts = exchange(parts, REST)
    (parts,) = call(total_kernel, [shape((BLOCKS, SHARD, CHANS), bf16)], parts)
    sums = exchange(parts, PLANE)
    d_feat, gmix, grad_r = call(
        post_kernel,
        [shape((1, ATOMS, CHANS), f32), shape((3 * CHANS, CHANS), f32), shape((NB, CHANS), f32)],
        dext, gain, sends, *near, far, sums,
    )
    return d_feat, gmix, grad_r


def solution(mesh):
    fine = Mesh(mesh.devices.reshape(4, 4, 4, 2, 4), DOM + ("rep",))
    in_specs = (
        P("rep", DOM, None),
        P("rep", DOM),
        P(),
        P("rep", None, DOM),
        P("rep", DOM),
        P("rep", DOM),
        P("rep", None, DOM),
        P(),
        P(),
        P("rep", DOM, None),
    )
    out_specs = (P("rep", DOM, None), P(), P())
    return jax.shard_map(
        on_device, mesh=fine, in_specs=in_specs, out_specs=out_specs, check_vma=False
    )
```

```python
import jax
import jax.numpy as jnp
import numpy as np
from jax import lax
from jax.experimental import pallas as pl
from jax.experimental.pallas import tpu as pltpu
from jax.sharding import Mesh, PartitionSpec as P

msg_scale = 0.35
cutoff = 6.0
clip_norm = 256.0
f32, bf16 = jnp.float32, jnp.bfloat16

CHANS = 128
NB = 8
ATOMS = 64
FACES = 6
PAD = 32
GHOST = 24
ROWS = ATOMS + FACES * PAD
EDGES = 4096
CHUNK = 1024
SHARD = 16
RING = 16
PLANE = ("zl", "x", "core")
PEERS = 32
REST = ("y", "rep")
OTHERS = 16
DOM = ("zl", "x", "y", "core")
STRIDES = (1, -1, 4, -4)
HIGH = lax.Precision.HIGHEST


def dot(a, b, dims, precision=None):
    return lax.dot_general(
        a, b, (dims, ((), ())), precision=precision, preferred_element_type=f32
    )


def rows_iota(shape):
    return lax.broadcasted_iota(jnp.int32, shape, 0)


def call(kernel, outs, *args, scratch=(), cost=None, space=pltpu.VMEM, limit=32):
    return pl.pallas_call(
        kernel,
        out_shape=outs,
        in_specs=[pl.BlockSpec(memory_space=space) for _ in args],
        out_specs=[pl.BlockSpec(memory_space=pltpu.VMEM) for _ in outs],
        scratch_shapes=list(scratch),
        cost_estimate=cost,
        compiler_params=pltpu.CompilerParams(vmem_limit_bytes=limit * 1024 * 1024),
    )(*args)


def position():
    ring = lax.axis_index("zl") * 4 + lax.axis_index("x")
    return ring, lax.axis_index("core")


def peer(ring, stride, core):
    return lax.rem(ring + stride + RING, RING) * 2 + core


def pre_kernel(
    feat_hbm, species_hbm, gain_hbm, sends_hbm, own_ref, gain_out, next_ref, pick_ref,
    feat_ref, species_ref, gain_ref, sends_ref, sems,
):
    copies = [
        pltpu.make_async_copy(src, dst, sems.at[i])
        for i, (src, dst) in enumerate(
            [
                (feat_hbm, feat_ref),
                (species_hbm, species_ref),
                (gain_hbm, gain_ref),
                (sends_hbm, sends_ref),
            ]
        )
    ]
    for copy in copies:
        copy.start()
    pick_ref[...] = jnp.zeros_like(pick_ref)
    for copy in copies:
        copy.wait()
    hot = (rows_iota((8, ATOMS)) == species_ref[...]).astype(f32)
    gains = jnp.concatenate([gain_ref[...], jnp.zeros((3, CHANS), f32)], axis=0)
    gain = dot(hot, gains, ((0,), (0,)), HIGH)
    own = (feat_ref[0].astype(f32) * gain).astype(bf16)
    own_ref[...] = own
    gain_out[...] = gain
    ring, core = position()
    picked = []
    for face in range(FACES):
        hot = (rows_iota((ATOMS, GHOST)) == sends_ref[face]).astype(f32)
        hot = jnp.concatenate([hot, jnp.zeros((ATOMS, PAD - GHOST), f32)], axis=1)
        picked.append(dot(hot.astype(bf16), own, ((0,), (0,))))
    next_ref[...] = jnp.where(core == 0, picked[1], picked[0]).astype(bf16)
    pick_ref[peer(ring, 0, 1 - core)] = jnp.where(core == 0, picked[0], picked[1]).astype(bf16)
    for stride, block in zip(STRIDES, picked[2:]):
        pick_ref[peer(ring, stride, core)] = block.astype(bf16)


def prep_kernel(
    vec_ref, src_ref, dst_ref, wrad_ref, hot_ref, harm_ref, radial_ref, basis_ref, harm_s, basis_s
):
    geometry(vec_ref, harm_s, basis_s)
    w_top, w_low = split(wrad_ref[...])
    wrad = jnp.concatenate([w_top, w_low, w_top], axis=0).T.astype(bf16)
    for start in range(0, EDGES, CHUNK):
        at = pl.ds(start, CHUNK)
        src = src_ref[:, at]
        shift = jnp.zeros_like(src)
        for face in range(1, FACES):
            shift = shift + jnp.where(src >= ATOMS + face * GHOST, PAD - GHOST, 0)
        hot = jnp.where(rows_iota((ROWS, CHUNK)) == src + shift, 1.0, 0.0)
        hot_ref[:, at] = hot.astype(bf16)
        b_top, b_low = split(basis_s[:, at])
        basis = jnp.concatenate([b_top, b_top, b_low], axis=0).astype(bf16)
        radial_ref[:, at] = dot(wrad, basis, ((1,), (0,)))
        basis_ref[:, at] = jnp.concatenate([b_top, b_low], axis=0).astype(bf16)
        own_hot = rows_iota((ATOMS, CHUNK)) == dst_ref[:, at]
        harm_ref[0:ATOMS, at] = jnp.where(own_hot, 1.0, 0.0).astype(bf16)
        for k in range(1, 9):
            harm = harm_s[k : k + 1, at]
            harm_ref[k * ATOMS : (k + 1) * ATOMS, at] = jnp.where(own_hot, harm, 0.0).astype(bf16)


def geometry(vec_ref, harm_ref, basis_ref):
    vx, vy, vz = (vec_ref[i] for i in range(3))
    square = vx * vx + vy * vy + vz * vz + 0.25
    inv_r = lax.rsqrt(square)
    radius = square * inv_r
    ux, uy, uz = vx * inv_r, vy * inv_r, vz * inv_r
    r3, r5, r15 = 3.0**0.5, 5.0**0.5, 15.0**0.5
    harms = [
        jnp.ones_like(ux),
        r3 * ux,
        r3 * uy,
        r3 * uz,
        r15 * ux * uy,
        r15 * uy * uz,
        0.5 * r5 * (3.0 * uz * uz - 1.0),
        r15 * ux * uz,
        0.5 * r15 * (ux * ux - uy * uy),
    ]
    for k, h in enumerate(harms):
        harm_ref[k : k + 1, :] = h
    scaled = radius * (1.0 / cutoff)
    envelope = 1.0 - scaled * scaled
    envelope = envelope * envelope * inv_r
    t = scaled * np.float32(np.pi) - np.float32(np.pi / 2)
    t2 = t * t
    sin_t = series(t2, 1) * t
    cos_t = series(t2, 0)
    twice = -2.0 * sin_t
    before, now = jnp.zeros_like(t), cos_t * envelope
    for b in range(NB):
        basis_ref[b : b + 1, :] = now
        before, now = now, twice * now - before


def series(square, odd):
    terms = [(-1.0) ** n / float(np.prod(np.arange(1, 2 * n + odd + 1.0))) for n in range(9)]
    total = jnp.full_like(square, terms[-1])
    for term in terms[-2::-1]:
        total = total * square + term
    return total


def split(values):
    top = values.astype(bf16).astype(f32)
    return top, values - top


def main_kernel(
    own_ref, next_ref, got_ref, hot_ref, harm_ref, radial_ref, basis_ref, wmix_ref, cot_ref,
    dext_ref, back_ref, send_ref,
    source_s, mom_s, dmom_s,
):
    ring, core = position()
    near = got_ref[peer(ring, 0, 1 - core)].astype(f32)
    other = next_ref[...].astype(f32)
    blocks = [own_ref[...].astype(f32)]
    blocks += [jnp.where(core == 0, other, near), jnp.where(core == 0, near, other)]
    for stride in STRIDES:
        blocks.append(got_ref[peer(ring, -stride, core)].astype(f32))
    ext = jnp.concatenate(blocks, axis=0).T.astype(bf16)
    mom_s[...] = jnp.zeros_like(mom_s)
    for start in range(0, EDGES, CHUNK):
        at = pl.ds(start, CHUNK)
        source = dot(ext, hot_ref[:, at], ((1,), (0,)))
        source_s[:, at] = source.astype(bf16)
        message = (radial_ref[:, at] * source).astype(bf16)
        mom_s[...] += dot(harm_ref[:, at], message, ((1,), (1,)))
    moments = [msg_scale * mom_s[k * ATOMS : (k + 1) * ATOMS, :] for k in range(9)]
    squares = [m * m for m in moments]
    two = squares[4]
    for k in range(5, 9):
        two = two + squares[k]
    inv = jnp.concatenate([squares[0], squares[1] + squares[2] + squares[3], two], axis=1).astype(bf16)
    pre = dot(inv, wmix_ref[...], ((1,), (0,)))
    sigma = jax.nn.sigmoid(pre)
    slope = sigma * (1.0 + pre * (1.0 - sigma))
    dpre = (cot_ref[0].astype(f32) * slope).astype(bf16)
    gmix = dot(inv, dpre, ((0,), (0,))).astype(bf16)
    for i in range(3 * CHANS // SHARD):
        send_ref[i, 0:SHARD] = gmix[i * SHARD : (i + 1) * SHARD]
    dinv = dot(dpre, wmix_ref[...], ((1,), (1,)))
    groups = [0, 1, 1, 1, 2, 2, 2, 2, 2]
    for k in range(9):
        part = dinv[:, groups[k] * CHANS : (groups[k] + 1) * CHANS]
        mom_s[k * ATOMS : (k + 1) * ATOMS, :] = (2.0 * msg_scale) * moments[k] * part
    dmom_s[...] = mom_s[...].T.astype(bf16)
    dext = jnp.zeros((ROWS, CHANS), f32)
    gradr = jnp.zeros((2 * NB, CHANS), f32)
    for start in range(0, EDGES, CHUNK):
        at = pl.ds(start, CHUNK)
        dmsg = dot(dmom_s[...], harm_ref[:, at], ((1,), (0,)))
        dradial = dmsg * source_s[:, at].astype(f32)
        dsource = (dmsg * radial_ref[:, at]).astype(bf16)
        dext = dext + dot(hot_ref[:, at], dsource, ((1,), (1,)))
        gradr = gradr + dot(basis_ref[:, at], dradial.astype(bf16), ((1,), (1,)))
    gradr = jnp.concatenate([gradr[:NB] + gradr[NB:], jnp.zeros((SHARD - NB, CHANS), f32)], axis=0)
    send_ref[3 * CHANS // SHARD, 0:SHARD] = gradr.astype(bf16)
    for i in range(3 * CHANS // SHARD + 1, PEERS):
        send_ref[i, 0:SHARD] = jnp.zeros((SHARD, CHANS), bf16)
    for i in range(PEERS):
        send_ref[i, SHARD:] = jnp.zeros((PAD, CHANS), bf16)
    dext_ref[...] = dext[:ATOMS]
    ghosts = [dext[ATOMS + face * PAD : ATOMS + (face + 1) * PAD] for face in range(FACES)]
    back_ref[...] = jnp.where(core == 0, ghosts[0], ghosts[1]).astype(bf16)
    near = jnp.where(core == 0, ghosts[1], ghosts[0])
    send_ref[peer(ring, 0, 1 - core), SHARD:] = near.astype(bf16)
    for stride, block in zip(STRIDES, ghosts[2:]):
        send_ref[peer(ring, -stride, core), SHARD:] = block.astype(bf16)


def total_kernel(parts_ref, out_ref):
    total = parts_ref[0, :SHARD].astype(f32)
    for i in range(1, parts_ref.shape[0]):
        total = total + parts_ref[i, :SHARD].astype(f32)
    total = total.astype(bf16)
    for i in range(out_ref.shape[0]):
        out_ref[i] = total


def post_kernel(
    dext_ref, gain_ref, sends_ref, next_ref, got_ref, sums_ref, dfeat_ref, gmix_ref, grad_ref
):
    ring, core = position()
    near = got_ref[peer(ring, 0, 1 - core), SHARD:].astype(f32)
    other = next_ref[...].astype(f32)
    blocks = [jnp.where(core == 0, near, other), jnp.where(core == 0, other, near)]
    for stride in STRIDES:
        blocks.append(got_ref[peer(ring, stride, core), SHARD:].astype(f32))
    total = dext_ref[...]
    for face in range(FACES):
        hot = (rows_iota((ATOMS, GHOST)) == sends_ref[face]).astype(f32)
        values = blocks[face][:GHOST].astype(bf16)
        total = total + dot(hot.astype(bf16), values, ((1,), (0,)))
    dfeat_ref[0] = total * gain_ref[...]
    whole = 3 * CHANS // SHARD
    parts = [sums_ref[i].astype(f32) for i in range(whole)]
    grad = sums_ref[whole].astype(f32)[:NB]
    square = grad * grad
    for part in parts:
        for i in range(0, SHARD, NB):
            square = square + part[i : i + NB] * part[i : i + NB]
    norm = jnp.sqrt(jnp.sum(square, keepdims=True))
    factor = clip_norm / jnp.maximum(norm, clip_norm)
    for i, part in enumerate(parts):
        gmix_ref[i * SHARD : (i + 1) * SHARD, :] = factor * part
    grad_ref[...] = factor * grad


def swap(block):
    pairs = []
    for i in range(1, 128, 2):
        j = (i + 1) % 128
        pairs += [(i, j), (j, i)]
    return lax.ppermute(block, DOM, pairs)


def exchange(blocks, axes):
    return lax.all_to_all(blocks, axes, 0, 0, tiled=True)


def on_device(feat, species, species_gain, send_lists, edge_src, edge_dst, edge_vec, w_rad, w_mix, out_cot):
    shape = jax.ShapeDtypeStruct
    sends = send_lists.reshape(FACES, 1, GHOST)
    own, gain, block, picks = call(
        pre_kernel,
        [
            shape((ATOMS, CHANS), bf16),
            shape((ATOMS, CHANS), f32),
            shape((PAD, CHANS), bf16),
            shape((PEERS, PAD, CHANS), bf16),
        ],
        feat, species, species_gain, sends,
        scratch=[
            pltpu.VMEM((1, ATOMS, CHANS), bf16),
            pltpu.VMEM((1, ATOMS), jnp.int32),
            pltpu.VMEM((5, CHANS), f32),
            pltpu.VMEM((FACES, 1, GHOST), jnp.int32),
            pltpu.SemaphoreType.DMA((4,)),
        ],
        space=pl.ANY,
        limit=60,
    )
    near = swap(block)
    far = exchange(picks, PLANE)
    edges = call(
        prep_kernel,
        [
            shape((ROWS, EDGES), bf16),
            shape((9 * ATOMS, EDGES), bf16),
            shape((CHANS, EDGES), f32),
            shape((2 * NB, EDGES), bf16),
        ],
        edge_vec.reshape(3, 1, EDGES), edge_src, edge_dst, w_rad,
        scratch=[pltpu.VMEM((16, EDGES), f32), pltpu.VMEM((NB, EDGES), f32)],
        cost=pl.CostEstimate(flops=2000000000, bytes_accessed=9000000, transcendentals=0),
    )
    dext, block, blocks = call(
        main_kernel,
        [
            shape((ATOMS, CHANS), f32),
            shape((PAD, CHANS), bf16),
            shape((PEERS, SHARD + PAD, CHANS), bf16),
        ],
        own, near, far, *edges, w_mix, out_cot,
        scratch=[
            pltpu.VMEM((CHANS, EDGES), bf16),
            pltpu.VMEM((9 * ATOMS, CHANS), f32),
            pltpu.VMEM((CHANS, 9 * ATOMS), bf16),
        ],
    )
    near = swap(block)
    far = exchange(blocks, PLANE)
    (parts,) = call(total_kernel, [shape((OTHERS, SHARD, CHANS), bf16)], far)
    parts = exchange(parts, REST)
    (parts,) = call(total_kernel, [shape((PEERS, SHARD, CHANS), bf16)], parts)
    sums = exchange(parts, PLANE)
    d_feat, gmix, grad_r = call(
        post_kernel,
        [shape((1, ATOMS, CHANS), f32), shape((3 * CHANS, CHANS), f32), shape((NB, CHANS), f32)],
        dext, gain, sends, near, far, sums,
    )
    return d_feat, gmix, grad_r


def solution(mesh):
    fine = Mesh(mesh.devices.reshape(4, 4, 4, 2, 4), DOM + ("rep",))
    in_specs = (
        P("rep", DOM, None),
        P("rep", DOM),
        P(),
        P("rep", None, DOM),
        P("rep", DOM),
        P("rep", DOM),
        P("rep", None, DOM),
        P(),
        P(),
        P("rep", DOM, None),
    )
    out_specs = (P("rep", DOM, None), P(), P())
    return jax.shard_map(
        on_device, mesh=fine, in_specs=in_specs, out_specs=out_specs, check_vma=False
    )
```

```python
import jax
import jax.numpy as jnp
import numpy as np
from jax import lax
from jax.experimental import pallas as pl
from jax.experimental.pallas import tpu as pltpu
from jax.sharding import Mesh, PartitionSpec as P

msg_scale = 0.35
cutoff = 6.0
clip_norm = 256.0
f32, bf16 = jnp.float32, jnp.bfloat16

CHANS = 128
NB = 8
ATOMS = 64
FACES = 6
PAD = 32
GHOST = 24
ROWS = ATOMS + FACES * PAD
EDGES = 4096
CHUNK = 1024
SHARD = 16
RING = 16
PLANE = ("zl", "x", "core")
PEERS = 32
SLAB = ("x", "y", "core")
LINE = ("zl", "rep")
LINES = 16
MOVES = (-1, 1, -8, 8)
DOM = ("zl", "x", "y", "core")
STRIDES = (1, -1, 4, -4)
HIGH = lax.Precision.HIGHEST


def dot(a, b, dims, precision=None):
    return lax.dot_general(
        a, b, (dims, ((), ())), precision=precision, preferred_element_type=f32
    )


def rows_iota(shape):
    return lax.broadcasted_iota(jnp.int32, shape, 0)


def call(kernel, outs, *args, scratch=(), cost=None, space=pltpu.VMEM, limit=48):
    return pl.pallas_call(
        kernel,
        out_shape=outs,
        in_specs=[pl.BlockSpec(memory_space=space) for _ in args],
        out_specs=[pl.BlockSpec(memory_space=pltpu.VMEM) for _ in outs],
        scratch_shapes=list(scratch),
        cost_estimate=cost,
        compiler_params=pltpu.CompilerParams(vmem_limit_bytes=limit * 1024 * 1024),
    )(*args)


def position():
    ring = lax.axis_index("zl") * 4 + lax.axis_index("x")
    return ring, lax.axis_index("core")


def peer(ring, stride, core):
    return lax.rem(ring + stride + RING, RING) * 2 + core


def pre_kernel(
    feat_hbm, species_hbm, gain_hbm, sends_hbm, own_ref, gain_out, next_ref, pick_ref,
    feat_ref, species_ref, gain_ref, sends_ref, sems,
):
    copies = [
        pltpu.make_async_copy(src, dst, sems.at[i])
        for i, (src, dst) in enumerate(
            [
                (feat_hbm, feat_ref),
                (species_hbm, species_ref),
                (gain_hbm, gain_ref),
                (sends_hbm, sends_ref),
            ]
        )
    ]
    for copy in copies:
        copy.start()
    pick_ref[...] = jnp.zeros_like(pick_ref)
    for copy in copies:
        copy.wait()
    hot = (rows_iota((8, ATOMS)) == species_ref[...]).astype(f32)
    gains = jnp.concatenate([gain_ref[...], jnp.zeros((3, CHANS), f32)], axis=0)
    gain = dot(hot, gains, ((0,), (0,)), HIGH)
    own = (feat_ref[0].astype(f32) * gain).astype(bf16)
    own_ref[...] = own
    gain_out[...] = gain
    ring, core = position()
    picked = []
    for face in range(FACES):
        hot = (rows_iota((ATOMS, GHOST)) == sends_ref[face]).astype(f32)
        hot = jnp.concatenate([hot, jnp.zeros((ATOMS, PAD - GHOST), f32)], axis=1)
        picked.append(dot(hot.astype(bf16), own, ((0,), (0,))))
    next_ref[...] = jnp.where(core == 0, picked[1], picked[0]).astype(bf16)
    pick_ref[peer(ring, 0, 1 - core)] = jnp.where(core == 0, picked[0], picked[1]).astype(bf16)
    for stride, block in zip(STRIDES, picked[2:]):
        pick_ref[peer(ring, stride, core)] = block.astype(bf16)


def geo_kernel(vec_ref, harm_ref, basis_ref):
    vx, vy, vz = (vec_ref[i] for i in range(3))
    square = vx * vx + vy * vy + vz * vz + 0.25
    inv_r = lax.rsqrt(square)
    radius = square * inv_r
    ux, uy, uz = vx * inv_r, vy * inv_r, vz * inv_r
    r3, r5, r15 = 3.0**0.5, 5.0**0.5, 15.0**0.5
    harms = [
        jnp.ones_like(ux),
        r3 * ux,
        r3 * uy,
        r3 * uz,
        r15 * ux * uy,
        r15 * uy * uz,
        0.5 * r5 * (3.0 * uz * uz - 1.0),
        r15 * ux * uz,
        0.5 * r15 * (ux * ux - uy * uy),
    ]
    for k, h in enumerate(harms):
        harm_ref[k : k + 1, :] = h
    scaled = radius * (1.0 / cutoff)
    envelope = 1.0 - scaled * scaled
    envelope = envelope * envelope * inv_r
    t = scaled * np.float32(np.pi) - np.float32(np.pi / 2)
    t2 = t * t
    sin_t = series(t2, 1) * t
    cos_t = series(t2, 0)
    twice = -2.0 * sin_t
    before, now = jnp.zeros_like(t), cos_t * envelope
    for b in range(NB):
        basis_ref[b : b + 1, :] = now
        before, now = now, twice * now - before


def series(square, odd):
    terms = [(-1.0) ** n / float(np.prod(np.arange(1, 2 * n + odd + 1.0))) for n in range(9)]
    total = jnp.full_like(square, terms[-1])
    for term in terms[-2::-1]:
        total = total * square + term
    return total


def split(values):
    top = values.astype(bf16).astype(f32)
    return top, values - top


def main_kernel(
    own_ref, next_ref, got_ref, src_ref, dst_ref, harm_ref, basis_ref, wrad_ref, wmix_ref, cot_ref,
    dext_ref, line_ref, send_ref,
    hot_s, harm_s, radial_s, source_s, mom_s, dmom_s,
):
    ring, core = position()
    near = got_ref[peer(ring, 0, 1 - core)].astype(f32)
    other = next_ref[...].astype(f32)
    blocks = [own_ref[...].astype(f32)]
    blocks += [jnp.where(core == 0, other, near), jnp.where(core == 0, near, other)]
    for stride in STRIDES:
        blocks.append(got_ref[peer(ring, -stride, core)].astype(f32))
    ext = jnp.concatenate(blocks, axis=0).T.astype(bf16)
    w_top, w_low = split(wrad_ref[...])
    wrad = jnp.concatenate([w_top, w_low, w_top], axis=0).T.astype(bf16)
    mom_s[...] = jnp.zeros_like(mom_s)
    for start in range(0, EDGES, CHUNK):
        at = pl.ds(start, CHUNK)
        src = src_ref[:, at]
        shift = jnp.zeros_like(src)
        for face in range(1, FACES):
            shift = shift + jnp.where(src >= ATOMS + face * GHOST, PAD - GHOST, 0)
        hot = jnp.where(rows_iota((ROWS, CHUNK)) == src + shift, 1.0, 0.0).astype(bf16)
        hot_s[:, at] = hot
        source = dot(ext, hot, ((1,), (0,)))
        source_s[:, at] = source.astype(bf16)
        b_top, b_low = split(basis_ref[:, at])
        basis = jnp.concatenate([b_top, b_top, b_low], axis=0).astype(bf16)
        radial = dot(wrad, basis, ((1,), (0,)))
        radial_s[:, at] = radial
        message = (radial * source).astype(bf16)
        own_hot = rows_iota((ATOMS, CHUNK)) == dst_ref[:, at]
        harm_s[0:ATOMS, at] = jnp.where(own_hot, 1.0, 0.0).astype(bf16)
        for k in range(1, 9):
            harm = harm_ref[k : k + 1, at]
            harm_s[k * ATOMS : (k + 1) * ATOMS, at] = jnp.where(own_hot, harm, 0.0).astype(bf16)
        mom_s[...] += dot(harm_s[:, at], message, ((1,), (1,)))
    moments = [msg_scale * mom_s[k * ATOMS : (k + 1) * ATOMS, :] for k in range(9)]
    squares = [m * m for m in moments]
    two = squares[4]
    for k in range(5, 9):
        two = two + squares[k]
    inv = jnp.concatenate([squares[0], squares[1] + squares[2] + squares[3], two], axis=1).astype(bf16)
    pre = dot(inv, wmix_ref[...], ((1,), (0,)))
    sigma = jax.nn.sigmoid(pre)
    slope = sigma * (1.0 + pre * (1.0 - sigma))
    dpre = (cot_ref[0].astype(f32) * slope).astype(bf16)
    gmix = dot(inv, dpre, ((0,), (0,))).astype(bf16)
    for i in range(3 * CHANS // SHARD):
        send_ref[i, 0:SHARD] = gmix[i * SHARD : (i + 1) * SHARD]
    dinv = dot(dpre, wmix_ref[...], ((1,), (1,)))
    groups = [0, 1, 1, 1, 2, 2, 2, 2, 2]
    for k in range(9):
        part = dinv[:, groups[k] * CHANS : (groups[k] + 1) * CHANS]
        mom_s[k * ATOMS : (k + 1) * ATOMS, :] = (2.0 * msg_scale) * moments[k] * part
    dmom_s[...] = mom_s[...].T.astype(bf16)
    dext = jnp.zeros((ROWS, CHANS), f32)
    gradr = jnp.zeros((2 * NB, CHANS), f32)
    for start in range(0, EDGES, CHUNK):
        at = pl.ds(start, CHUNK)
        dmsg = dot(dmom_s[...], harm_s[:, at], ((1,), (0,)))
        dradial = dmsg * source_s[:, at].astype(f32)
        dsource = (dmsg * radial_s[:, at]).astype(bf16)
        dext = dext + dot(hot_s[:, at], dsource, ((1,), (1,)))
        b_top, b_low = split(basis_ref[:, at])
        basis = jnp.concatenate([b_top, b_low], axis=0).astype(bf16)
        gradr = gradr + dot(basis, dradial.astype(bf16), ((1,), (1,)))
    gradr = jnp.concatenate([gradr[:NB] + gradr[NB:], jnp.zeros((SHARD - NB, CHANS), f32)], axis=0)
    send_ref[3 * CHANS // SHARD, 0:SHARD] = gradr.astype(bf16)
    for i in range(3 * CHANS // SHARD + 1, PEERS):
        send_ref[i, 0:SHARD] = jnp.zeros((SHARD, CHANS), bf16)
    for i in range(PEERS):
        send_ref[i, SHARD:] = jnp.zeros((PAD, CHANS), bf16)
    dext_ref[...] = dext[:ATOMS]
    ghosts = [dext[ATOMS + face * PAD : ATOMS + (face + 1) * PAD] for face in range(FACES)]
    spot = place()
    for move, block in zip(MOVES, ghosts[:4]):
        send_ref[lax.rem(spot + move + PEERS, PEERS), SHARD:] = block.astype(bf16)
    line_ref[0] = ghosts[4].astype(bf16)
    line_ref[1] = ghosts[5].astype(bf16)


def place():
    return (lax.axis_index("x") * 4 + lax.axis_index("y")) * 2 + lax.axis_index("core")


def passed(got_ref):
    spot = place()
    return [got_ref[lax.rem(spot - move + PEERS, PEERS), SHARD:] for move in MOVES]


def add_up(parts_ref, out_ref):
    total = parts_ref[0, :SHARD].astype(f32)
    for i in range(1, parts_ref.shape[0]):
        total = total + parts_ref[i, :SHARD].astype(f32)
    total = total.astype(bf16)
    for i in range(out_ref.shape[0]):
        out_ref[i] = total


def slab_kernel(parts_ref, line_ref, out_ref, down_ref, up_ref):
    add_up(parts_ref, out_ref)
    blocks = passed(parts_ref)
    down_ref[0], up_ref[0] = line_ref[0], line_ref[1]
    down_ref[1], up_ref[1] = blocks[0], blocks[1]
    down_ref[2], up_ref[2] = blocks[2], blocks[3]


def line_kernel(parts_ref, out_ref):
    add_up(parts_ref, out_ref)


def post_kernel(
    dext_ref, gain_ref, sends_ref, got_ref, down_ref, up_ref, sums_ref, dfeat_ref, gmix_ref, grad_ref
):
    spot = place()
    local = passed(got_ref)
    blocks = []
    for move, block, other in zip(MOVES, local, (down_ref[1], up_ref[1], down_ref[2], up_ref[2])):
        crossed = spot - move >= PEERS if move < 0 else spot < move
        blocks.append(jnp.where(crossed, other.astype(f32), block.astype(f32)))
    blocks += [down_ref[0].astype(f32), up_ref[0].astype(f32)]
    total = dext_ref[...]
    for face in range(FACES):
        hot = (rows_iota((ATOMS, GHOST)) == sends_ref[face]).astype(f32)
        values = blocks[face][:GHOST].astype(bf16)
        total = total + dot(hot.astype(bf16), values, ((1,), (0,)))
    dfeat_ref[0] = total * gain_ref[...]
    whole = 3 * CHANS // SHARD
    parts = [sums_ref[i].astype(f32) for i in range(whole)]
    grad = sums_ref[whole].astype(f32)[:NB]
    square = grad * grad
    for part in parts:
        for i in range(0, SHARD, NB):
            square = square + part[i : i + NB] * part[i : i + NB]
    norm = jnp.sqrt(jnp.sum(square, keepdims=True))
    factor = clip_norm / jnp.maximum(norm, clip_norm)
    for i, part in enumerate(parts):
        gmix_ref[i * SHARD : (i + 1) * SHARD, :] = factor * part
    grad_ref[...] = factor * grad


def swap(block):
    pairs = []
    for i in range(1, 128, 2):
        j = (i + 1) % 128
        pairs += [(i, j), (j, i)]
    return lax.ppermute(block, DOM, pairs)


def exchange(blocks, axes):
    return lax.all_to_all(blocks, axes, 0, 0, tiled=True)


def on_device(feat, species, species_gain, send_lists, edge_src, edge_dst, edge_vec, w_rad, w_mix, out_cot):
    shape = jax.ShapeDtypeStruct
    sends = send_lists.reshape(FACES, 1, GHOST)
    own, gain, block, picks = call(
        pre_kernel,
        [
            shape((ATOMS, CHANS), bf16),
            shape((ATOMS, CHANS), f32),
            shape((PAD, CHANS), bf16),
            shape((PEERS, PAD, CHANS), bf16),
        ],
        feat, species, species_gain, sends,
        scratch=[
            pltpu.VMEM((1, ATOMS, CHANS), bf16),
            pltpu.VMEM((1, ATOMS), jnp.int32),
            pltpu.VMEM((5, CHANS), f32),
            pltpu.VMEM((FACES, 1, GHOST), jnp.int32),
            pltpu.SemaphoreType.DMA((4,)),
        ],
        space=pl.ANY,
        limit=60,
    )
    near = swap(block)
    far = exchange(picks, PLANE)
    harm, basis = call(
        geo_kernel,
        [shape((16, EDGES), f32), shape((NB, EDGES), f32)],
        edge_vec.reshape(3, 1, EDGES),
        cost=pl.CostEstimate(flops=1000000, bytes_accessed=400000, transcendentals=0),
    )
    dext, line, blocks = call(
        main_kernel,
        [
            shape((ATOMS, CHANS), f32),
            shape((2, PAD, CHANS), bf16),
            shape((PEERS, SHARD + PAD, CHANS), bf16),
        ],
        own, near, far, edge_src, edge_dst, harm, basis, w_rad, w_mix, out_cot,
        scratch=[
            pltpu.VMEM((ROWS, EDGES), bf16),
            pltpu.VMEM((9 * ATOMS, EDGES), bf16),
            pltpu.VMEM((CHANS, EDGES), f32),
            pltpu.VMEM((CHANS, EDGES), bf16),
            pltpu.VMEM((9 * ATOMS, CHANS), f32),
            pltpu.VMEM((CHANS, 9 * ATOMS), bf16),
        ],
    )
    far = exchange(blocks, SLAB)
    parts, down, up = call(
        slab_kernel,
        [shape((LINES, SHARD, CHANS), bf16)] + [shape((3, PAD, CHANS), bf16)] * 2,
        far, line,
    )
    down = lax.ppermute(down, "zl", [(i, (i + 3) % 4) for i in range(4)])
    up = lax.ppermute(up, "zl", [(i, (i + 1) % 4) for i in range(4)])
    parts = exchange(parts, LINE)
    (parts,) = call(line_kernel, [shape((PEERS, SHARD, CHANS), bf16)], parts)
    sums = exchange(parts, SLAB)
    d_feat, gmix, grad_r = call(
        post_kernel,
        [shape((1, ATOMS, CHANS), f32), shape((3 * CHANS, CHANS), f32), shape((NB, CHANS), f32)],
        dext, gain, sends, far, down, up, sums,
    )
    return d_feat, gmix, grad_r


def solution(mesh):
    fine = Mesh(mesh.devices.reshape(4, 4, 4, 2, 4), DOM + ("rep",))
    in_specs = (
        P("rep", DOM, None),
        P("rep", DOM),
        P(),
        P("rep", None, DOM),
        P("rep", DOM),
        P("rep", DOM),
        P("rep", None, DOM),
        P(),
        P(),
        P("rep", DOM, None),
    )
    out_specs = (P("rep", DOM, None), P(), P())
    return jax.shard_map(
        on_device, mesh=fine, in_specs=in_specs, out_specs=out_specs, check_vma=False
    )
```

```python
import jax
import jax.numpy as jnp
import numpy as np
from jax import lax
from jax.experimental import pallas as pl
from jax.experimental.pallas import tpu as pltpu
from jax.sharding import Mesh, PartitionSpec as P

msg_scale = 0.35
cutoff = 6.0
clip_norm = 256.0
f32, bf16 = jnp.float32, jnp.bfloat16

CHANS = 128
NB = 8
ATOMS = 64
FACES = 6
GHOST = 24
ROWS = ATOMS + FACES * GHOST
EDGES = 4096
CHUNK = 1024
SHARD = 16
RING = 16
PLANE = ("zl", "x")
PEERS = 32
SLAB = ("x", "y", "core")
LINE = ("zl", "rep")
LINES = 16
MOVES = (-1, 1, -8, 8)
DOM = ("zl", "x", "y", "core")
STRIDES = (1, -1, 4, -4)
HIGH = lax.Precision.HIGHEST


def dot(a, b, dims, precision=None):
    return lax.dot_general(
        a, b, (dims, ((), ())), precision=precision, preferred_element_type=f32
    )


def rows_iota(shape):
    return lax.broadcasted_iota(jnp.int32, shape, 0)


def call(kernel, outs, *args, scratch=(), cost=None, space=pltpu.VMEM, limit=48):
    return pl.pallas_call(
        kernel,
        out_shape=outs,
        in_specs=[pl.BlockSpec(memory_space=space) for _ in args],
        out_specs=[pl.BlockSpec(memory_space=pltpu.VMEM) for _ in outs],
        scratch_shapes=list(scratch),
        cost_estimate=cost,
        compiler_params=pltpu.CompilerParams(vmem_limit_bytes=limit * 1024 * 1024),
    )(*args)


def position():
    ring = lax.axis_index("zl") * 4 + lax.axis_index("x")
    return ring, lax.axis_index("core")


def peer(ring, stride):
    return lax.rem(ring + stride + RING, RING)


def pre_kernel(
    feat_hbm, species_hbm, gain_hbm, sends_hbm, own_ref, gain_out, pair_ref, pick_ref,
    feat_ref, species_ref, gain_ref, sends_ref, sems,
):
    copies = [
        pltpu.make_async_copy(src, dst, sems.at[i])
        for i, (src, dst) in enumerate(
            [
                (feat_hbm, feat_ref),
                (species_hbm, species_ref),
                (gain_hbm, gain_ref),
                (sends_hbm, sends_ref),
            ]
        )
    ]
    for copy in copies:
        copy.start()
    pick_ref[...] = jnp.zeros_like(pick_ref)
    for copy in copies:
        copy.wait()
    hot = (rows_iota((8, ATOMS)) == species_ref[...]).astype(f32)
    gains = jnp.concatenate([gain_ref[...], jnp.zeros((3, CHANS), f32)], axis=0)
    gain = dot(hot, gains, ((0,), (0,)), HIGH)
    own = (feat_ref[0].astype(f32) * gain).astype(bf16)
    own_ref[...] = own
    gain_out[...] = gain
    ring, core = position()
    for face in range(FACES):
        hot = (rows_iota((ATOMS, GHOST)) == sends_ref[face]).astype(f32)
        picked = dot(hot.astype(bf16), own, ((0,), (0,))).astype(bf16)
        if face < 2:
            pair_ref[lax.rem(core + face, 2)] = picked
        else:
            pick_ref[peer(ring, STRIDES[face - 2])] = picked


def geo_kernel(vec_ref, harm_ref, basis_ref):
    vx, vy, vz = (vec_ref[i] for i in range(3))
    square = vx * vx + vy * vy + vz * vz + 0.25
    inv_r = lax.rsqrt(square)
    radius = square * inv_r
    ux, uy, uz = vx * inv_r, vy * inv_r, vz * inv_r
    r3, r5, r15 = 3.0**0.5, 5.0**0.5, 15.0**0.5
    harms = [
        jnp.ones_like(ux),
        r3 * ux,
        r3 * uy,
        r3 * uz,
        r15 * ux * uy,
        r15 * uy * uz,
        0.5 * r5 * (3.0 * uz * uz - 1.0),
        r15 * ux * uz,
        0.5 * r15 * (ux * ux - uy * uy),
    ]
    for k, h in enumerate(harms):
        harm_ref[k : k + 1, :] = h
    scaled = radius * (1.0 / cutoff)
    envelope = 1.0 - scaled * scaled
    envelope = envelope * envelope * inv_r
    t = scaled * np.float32(np.pi) - np.float32(np.pi / 2)
    t2 = t * t
    sin_t = series(t2, 1) * t
    cos_t = series(t2, 0)
    twice = -2.0 * sin_t
    before, now = jnp.zeros_like(t), cos_t * envelope
    for b in range(NB):
        basis_ref[b : b + 1, :] = now
        before, now = now, twice * now - before


def series(square, odd):
    terms = [(-1.0) ** n / float(np.prod(np.arange(1, 2 * n + odd + 1.0))) for n in range(9)]
    total = jnp.full_like(square, terms[-1])
    for term in terms[-2::-1]:
        total = total * square + term
    return total


def split(values):
    top = values.astype(bf16).astype(f32)
    return top, values - top


def main_kernel(
    own_ref, p0, p1, got_ref, src_ref, dst_ref, harm_ref, basis_ref, wrad_ref, wmix_ref, cot_ref,
    dext_ref, line_ref, send_ref,
    hot_s, harm_s, radial_s, source_s, mom_s, dmom_s,
):
    ring, core = position()
    a, b = p0[...].astype(f32), p1[...].astype(f32)
    blocks = [own_ref[...].astype(f32), jnp.where(core == 0, b, a), jnp.where(core == 0, a, b)]
    for stride in STRIDES:
        blocks.append(got_ref[peer(ring, -stride)].astype(f32))
    ext = jnp.concatenate(blocks, axis=0).T.astype(bf16)
    w_top, w_low = split(wrad_ref[...])
    wrad = jnp.concatenate([w_top, w_low, w_top], axis=0).T.astype(bf16)
    mom_s[...] = jnp.zeros_like(mom_s)
    for start in range(0, EDGES, CHUNK):
        at = pl.ds(start, CHUNK)
        src = src_ref[:, at]
        hot = jnp.where(rows_iota((ROWS, CHUNK)) == src, 1.0, 0.0).astype(bf16)
        hot_s[:, at] = hot
        source = dot(ext, hot, ((1,), (0,)))
        source_s[:, at] = source.astype(bf16)
        b_top, b_low = split(basis_ref[:, at])
        basis = jnp.concatenate([b_top, b_top, b_low], axis=0).astype(bf16)
        radial = dot(wrad, basis, ((1,), (0,)))
        radial_s[:, at] = radial
        message = (radial * source).astype(bf16)
        own_hot = rows_iota((ATOMS, CHUNK)) == dst_ref[:, at]
        harm_s[0:ATOMS, at] = jnp.where(own_hot, 1.0, 0.0).astype(bf16)
        for k in range(1, 9):
            harm = harm_ref[k : k + 1, at]
            harm_s[k * ATOMS : (k + 1) * ATOMS, at] = jnp.where(own_hot, harm, 0.0).astype(bf16)
        mom_s[...] += dot(harm_s[:, at], message, ((1,), (1,)))
    moments = [msg_scale * mom_s[k * ATOMS : (k + 1) * ATOMS, :] for k in range(9)]
    squares = [m * m for m in moments]
    two = squares[4]
    for k in range(5, 9):
        two = two + squares[k]
    inv = jnp.concatenate([squares[0], squares[1] + squares[2] + squares[3], two], axis=1).astype(bf16)
    pre = dot(inv, wmix_ref[...], ((1,), (0,)))
    sigma = jax.nn.sigmoid(pre)
    slope = sigma * (1.0 + pre * (1.0 - sigma))
    dpre = (cot_ref[0].astype(f32) * slope).astype(bf16)
    gmix = dot(inv, dpre, ((0,), (0,)))
    nothing = jnp.zeros((GHOST, CHANS), f32)
    for i in range(3 * CHANS // SHARD):
        shard = gmix[i * SHARD : (i + 1) * SHARD]
        send_ref[i] = jnp.concatenate([shard, nothing], axis=0).astype(bf16)
    dinv = dot(dpre, wmix_ref[...], ((1,), (1,)))
    groups = [0, 1, 1, 1, 2, 2, 2, 2, 2]
    for k in range(9):
        part = dinv[:, groups[k] * CHANS : (groups[k] + 1) * CHANS]
        mom_s[k * ATOMS : (k + 1) * ATOMS, :] = (2.0 * msg_scale) * moments[k] * part
    dmom_s[...] = mom_s[...].T.astype(bf16)
    dext = jnp.zeros((ROWS, CHANS), f32)
    gradr = jnp.zeros((2 * NB, CHANS), f32)
    for start in range(0, EDGES, CHUNK):
        at = pl.ds(start, CHUNK)
        dmsg = dot(dmom_s[...], harm_s[:, at], ((1,), (0,)))
        dradial = dmsg * source_s[:, at].astype(f32)
        dsource = (dmsg * radial_s[:, at]).astype(bf16)
        dext = dext + dot(hot_s[:, at], dsource, ((1,), (1,)))
        b_top, b_low = split(basis_ref[:, at])
        basis = jnp.concatenate([b_top, b_low], axis=0).astype(bf16)
        gradr = gradr + dot(basis, dradial.astype(bf16), ((1,), (1,)))
    gradr = jnp.concatenate([gradr[:NB] + gradr[NB:], nothing, nothing[:NB]], axis=0)
    send_ref[3 * CHANS // SHARD] = gradr.astype(bf16)
    for i in range(3 * CHANS // SHARD + 1, PEERS):
        send_ref[i] = jnp.zeros((SHARD + GHOST, CHANS), bf16)
    dext_ref[...] = dext[:ATOMS]
    ghosts = [dext[ATOMS + face * GHOST : ATOMS + (face + 1) * GHOST] for face in range(FACES)]
    spot = place()
    for move, block in zip(MOVES, ghosts[:4]):
        to = lax.rem(spot + move + PEERS, PEERS)
        shard = send_ref[to].astype(f32)[:SHARD]
        send_ref[to] = jnp.concatenate([shard, block], axis=0).astype(bf16)
    line_ref[0] = ghosts[4].astype(bf16)
    line_ref[1] = ghosts[5].astype(bf16)


def place():
    return (lax.axis_index("x") * 4 + lax.axis_index("y")) * 2 + lax.axis_index("core")


def passed(got_ref):
    spot = place()
    return [got_ref[lax.rem(spot - move + PEERS, PEERS)].astype(f32)[SHARD:] for move in MOVES]


def add_up(parts_ref, out_ref):
    total = parts_ref[0].astype(f32)[:SHARD]
    for i in range(1, parts_ref.shape[0]):
        total = total + parts_ref[i].astype(f32)[:SHARD]
    total = total.astype(bf16)
    for i in range(out_ref.shape[0]):
        out_ref[i] = total


def slab_kernel(parts_ref, line_ref, out_ref, down_ref, up_ref):
    add_up(parts_ref, out_ref)
    blocks = passed(parts_ref)
    down_ref[0], up_ref[0] = line_ref[0], line_ref[1]
    down_ref[1], up_ref[1] = blocks[0].astype(bf16), blocks[1].astype(bf16)
    down_ref[2], up_ref[2] = blocks[2].astype(bf16), blocks[3].astype(bf16)


def line_kernel(parts_ref, down_ref, up_ref, out_ref):
    add_up(parts_ref, out_ref)


def feat_kernel(dext_ref, gain_ref, sends_ref, got_ref, down_ref, up_ref, dfeat_ref):
    spot = place()
    local = passed(got_ref)
    blocks = []
    for move, block, other in zip(MOVES, local, (down_ref[1], up_ref[1], down_ref[2], up_ref[2])):
        crossed = spot - move >= PEERS if move < 0 else spot < move
        blocks.append(jnp.where(crossed, other.astype(f32), block))
    blocks += [down_ref[0].astype(f32), up_ref[0].astype(f32)]
    total = dext_ref[...]
    for face in range(FACES):
        hot = (rows_iota((ATOMS, GHOST)) == sends_ref[face]).astype(f32)
        total = total + dot(hot.astype(bf16), blocks[face].astype(bf16), ((1,), (0,)))
    dfeat_ref[0] = total * gain_ref[...]


def post_kernel(sums_ref, gmix_ref, grad_ref):
    whole = 3 * CHANS // SHARD
    parts = [sums_ref[i].astype(f32) for i in range(whole)]
    grad = sums_ref[whole].astype(f32)[:NB]
    square = grad * grad
    for part in parts:
        for i in range(0, SHARD, NB):
            square = square + part[i : i + NB] * part[i : i + NB]
    norm = jnp.sqrt(jnp.sum(square, keepdims=True))
    factor = clip_norm / jnp.maximum(norm, clip_norm)
    for i, part in enumerate(parts):
        gmix_ref[i * SHARD : (i + 1) * SHARD, :] = factor * part
    grad_ref[...] = factor * grad


def swap(block, parity):
    pairs = []
    for i in range(parity, 128, 2):
        j = (i + 1) % 128
        pairs += [(i, j), (j, i)]
    return lax.ppermute(block, DOM, pairs)


def exchange(blocks, axes):
    return lax.all_to_all(blocks, axes, 0, 0, tiled=True)


def on_device(feat, species, species_gain, send_lists, edge_src, edge_dst, edge_vec, w_rad, w_mix, out_cot):
    shape = jax.ShapeDtypeStruct
    sends = send_lists.reshape(FACES, 1, GHOST)
    own, gain, pair, picks = call(
        pre_kernel,
        [
            shape((ATOMS, CHANS), bf16),
            shape((ATOMS, CHANS), f32),
            shape((2, GHOST, CHANS), bf16),
            shape((RING, GHOST, CHANS), bf16),
        ],
        feat, species, species_gain, sends,
        scratch=[
            pltpu.VMEM((1, ATOMS, CHANS), bf16),
            pltpu.VMEM((1, ATOMS), jnp.int32),
            pltpu.VMEM((5, CHANS), f32),
            pltpu.VMEM((FACES, 1, GHOST), jnp.int32),
            pltpu.SemaphoreType.DMA((4,)),
        ],
        space=pl.ANY,
        limit=60,
    )
    near = [swap(pair[q], q) for q in range(2)]
    far = exchange(picks, PLANE)
    harm, basis = call(
        geo_kernel,
        [shape((16, EDGES), f32), shape((NB, EDGES), f32)],
        edge_vec.reshape(3, 1, EDGES),
        cost=pl.CostEstimate(flops=1000000, bytes_accessed=400000, transcendentals=0),
    )
    dext, line, blocks = call(
        main_kernel,
        [
            shape((ATOMS, CHANS), f32),
            shape((2, GHOST, CHANS), bf16),
            shape((PEERS, SHARD + GHOST, CHANS), bf16),
        ],
        own, *near, far, edge_src, edge_dst, harm, basis, w_rad, w_mix, out_cot,
        scratch=[
            pltpu.VMEM((ROWS, EDGES), bf16),
            pltpu.VMEM((9 * ATOMS, EDGES), bf16),
            pltpu.VMEM((CHANS, EDGES), f32),
            pltpu.VMEM((CHANS, EDGES), bf16),
            pltpu.VMEM((9 * ATOMS, CHANS), f32),
            pltpu.VMEM((CHANS, 9 * ATOMS), bf16),
        ],
    )
    far = exchange(blocks, SLAB)
    parts, down, up = call(
        slab_kernel,
        [shape((LINES, SHARD, CHANS), bf16)] + [shape((3, GHOST, CHANS), bf16)] * 2,
        far, line,
    )
    down = lax.ppermute(down, "zl", [(i, (i + 3) % 4) for i in range(4)])
    up = lax.ppermute(up, "zl", [(i, (i + 1) % 4) for i in range(4)])
    parts = exchange(parts, LINE)
    (parts,) = call(line_kernel, [shape((PEERS, SHARD, CHANS), bf16)], parts, down, up)
    sums = exchange(parts, SLAB)
    (d_feat,) = call(
        feat_kernel,
        [shape((1, ATOMS, CHANS), f32)],
        dext, gain, sends, far, down, up,
        cost=pl.CostEstimate(flops=10000000, bytes_accessed=500000, transcendentals=0),
    )
    gmix, grad_r = call(
        post_kernel, [shape((3 * CHANS, CHANS), f32), shape((NB, CHANS), f32)], sums
    )
    return d_feat, gmix, grad_r


def solution(mesh):
    fine = Mesh(mesh.devices.reshape(4, 4, 4, 2, 4), DOM + ("rep",))
    in_specs = (
        P("rep", DOM, None),
        P("rep", DOM),
        P(),
        P("rep", None, DOM),
        P("rep", DOM),
        P("rep", DOM),
        P("rep", None, DOM),
        P(),
        P(),
        P("rep", DOM, None),
    )
    out_specs = (P("rep", DOM, None), P(), P())
    return jax.shard_map(
        on_device, mesh=fine, in_specs=in_specs, out_specs=out_specs, check_vma=False
    )
```

```python
import jax
import jax.numpy as jnp
import numpy as np
from jax import lax
from jax.experimental import pallas as pl
from jax.experimental.pallas import tpu as pltpu
from jax.sharding import Mesh, PartitionSpec as P

msg_scale = 0.35
cutoff = 6.0
clip_norm = 256.0
f32, bf16 = jnp.float32, jnp.bfloat16

CHANS = 128
NB = 8
ATOMS = 64
FACES = 6
GHOST = 24
ROWS = ATOMS + FACES * GHOST
EDGES = 4096
CHUNK = 1024
SHARD = 16
RING = 16
PLANE = ("zl", "x")
PEERS = 32
SLAB = ("x", "y", "core")
LINE = ("zl", "rep")
LINES = 16
MOVES = (-1, 1, -8, 8)
DOM = ("zl", "x", "y", "core")
STRIDES = (1, -1, 4, -4)
HIGH = lax.Precision.HIGHEST


def dot(a, b, dims, precision=None):
    return lax.dot_general(
        a, b, (dims, ((), ())), precision=precision, preferred_element_type=f32
    )


def rows_iota(shape):
    return lax.broadcasted_iota(jnp.int32, shape, 0)


def call(kernel, outs, *args, scratch=(), cost=None, space=pltpu.VMEM, limit=48):
    return pl.pallas_call(
        kernel,
        out_shape=outs,
        in_specs=[pl.BlockSpec(memory_space=space) for _ in args],
        out_specs=[pl.BlockSpec(memory_space=pltpu.VMEM) for _ in outs],
        scratch_shapes=list(scratch),
        cost_estimate=cost,
        compiler_params=pltpu.CompilerParams(vmem_limit_bytes=limit * 1024 * 1024),
    )(*args)


def position():
    ring = lax.axis_index("zl") * 4 + lax.axis_index("x")
    return ring, lax.axis_index("core")


def peer(ring, stride):
    return lax.rem(ring + stride + RING, RING)


def pre_kernel(
    feat_hbm, species_hbm, gain_hbm, sends_hbm, own_ref, gain_out, pair_ref, pick_ref,
    feat_ref, species_ref, gain_ref, sends_ref, sems,
):
    copies = [
        pltpu.make_async_copy(src, dst, sems.at[i])
        for i, (src, dst) in enumerate(
            [
                (feat_hbm, feat_ref),
                (species_hbm, species_ref),
                (gain_hbm, gain_ref),
                (sends_hbm, sends_ref),
            ]
        )
    ]
    for copy in copies:
        copy.start()
    pick_ref[...] = jnp.zeros_like(pick_ref)
    for copy in copies:
        copy.wait()
    hot = (rows_iota((8, ATOMS)) == species_ref[...]).astype(f32)
    gains = jnp.concatenate([gain_ref[...], jnp.zeros((3, CHANS), f32)], axis=0)
    gain = dot(hot, gains, ((0,), (0,)), HIGH)
    own = (feat_ref[0].astype(f32) * gain).astype(bf16)
    own_ref[...] = own
    gain_out[...] = gain
    ring, core = position()
    for face in range(FACES):
        hot = (rows_iota((ATOMS, GHOST)) == sends_ref[face]).astype(f32)
        picked = dot(hot.astype(bf16), own, ((0,), (0,))).astype(bf16)
        if face < 2:
            pair_ref[lax.rem(core + face, 2)] = picked
        else:
            pick_ref[peer(ring, STRIDES[face - 2])] = picked


def geo_kernel(vec_ref, harm_ref, basis_ref):
    vx, vy, vz = (vec_ref[i] for i in range(3))
    square = vx * vx + vy * vy + vz * vz + 0.25
    inv_r = lax.rsqrt(square)
    radius = square * inv_r
    ux, uy, uz = vx * inv_r, vy * inv_r, vz * inv_r
    r3, r5, r15 = 3.0**0.5, 5.0**0.5, 15.0**0.5
    harms = [
        jnp.ones_like(ux),
        r3 * ux,
        r3 * uy,
        r3 * uz,
        r15 * ux * uy,
        r15 * uy * uz,
        0.5 * r5 * (3.0 * uz * uz - 1.0),
        r15 * ux * uz,
        0.5 * r15 * (ux * ux - uy * uy),
    ]
    for k, h in enumerate(harms):
        harm_ref[k : k + 1, :] = h
    scaled = radius * (1.0 / cutoff)
    envelope = 1.0 - scaled * scaled
    envelope = envelope * envelope * inv_r
    t = scaled * np.float32(np.pi) - np.float32(np.pi / 2)
    t2 = t * t
    sin_t = series(t2, 1) * t
    cos_t = series(t2, 0)
    twice = -2.0 * sin_t
    before, now = jnp.zeros_like(t), cos_t * envelope
    for b in range(NB):
        basis_ref[b : b + 1, :] = now
        before, now = now, twice * now - before


def series(square, odd):
    terms = [(-1.0) ** n / float(np.prod(np.arange(1, 2 * n + odd + 1.0))) for n in range(9)]
    total = jnp.full_like(square, terms[-1])
    for term in terms[-2::-1]:
        total = total * square + term
    return total


def split(values):
    top = values.astype(bf16).astype(f32)
    return top, values - top


def main_kernel(
    own_ref, p0, p1, got_ref, src_ref, dst_ref, harm_ref, basis_ref, wrad_ref, wmix_ref, cot_ref,
    dext_ref, line_ref, send_ref,
    hot_s, harm_s, radial_s, source_s, mom_s, dmom_s,
):
    ring, core = position()
    a, b = p0[...].astype(f32), p1[...].astype(f32)
    blocks = [own_ref[...].astype(f32), jnp.where(core == 0, b, a), jnp.where(core == 0, a, b)]
    for stride in STRIDES:
        blocks.append(got_ref[peer(ring, -stride)].astype(f32))
    ext = jnp.concatenate(blocks, axis=0).T.astype(bf16)
    w_top, w_low = split(wrad_ref[...])
    wrad = jnp.concatenate([w_top, w_low, w_top], axis=0).T.astype(bf16)
    turned = jnp.zeros((CHANS, 9 * ATOMS), f32)
    for start in range(0, EDGES, CHUNK):
        at = pl.ds(start, CHUNK)
        src = src_ref[:, at]
        hot = jnp.where(rows_iota((ROWS, CHUNK)) == src, 1.0, 0.0).astype(bf16)
        hot_s[:, at] = hot
        source = dot(ext, hot, ((1,), (0,)))
        source_s[:, at] = source.astype(bf16)
        b_top, b_low = split(basis_ref[:, at])
        basis = jnp.concatenate([b_top, b_top, b_low], axis=0).astype(bf16)
        radial = dot(wrad, basis, ((1,), (0,)))
        radial_s[:, at] = radial
        message = (radial * source).astype(bf16)
        own_hot = rows_iota((ATOMS, CHUNK)) == dst_ref[:, at]
        own_hot = jnp.where(own_hot, 1.0, 0.0).astype(bf16)
        harm_s[0:ATOMS, at] = own_hot
        for k in range(1, 9):
            harm = harm_ref[k : k + 1, at]
            harm_s[k * ATOMS : (k + 1) * ATOMS, at] = own_hot * harm.astype(bf16)
        turned = turned + dot(message, harm_s[:, at], ((1,), (1,)))
    mom_s[...] = turned.T
    moments = [msg_scale * mom_s[k * ATOMS : (k + 1) * ATOMS, :] for k in range(9)]
    squares = [m * m for m in moments]
    two = squares[4]
    for k in range(5, 9):
        two = two + squares[k]
    inv = jnp.concatenate([squares[0], squares[1] + squares[2] + squares[3], two], axis=1).astype(bf16)
    pre = dot(inv, wmix_ref[...], ((1,), (0,)))
    sigma = jax.nn.sigmoid(pre)
    slope = sigma * (1.0 + pre * (1.0 - sigma))
    dpre = (cot_ref[0].astype(f32) * slope).astype(bf16)
    gmix = dot(inv, dpre, ((0,), (0,)))
    nothing = jnp.zeros((GHOST, CHANS), f32)
    for i in range(3 * CHANS // SHARD):
        shard = gmix[i * SHARD : (i + 1) * SHARD]
        send_ref[i] = jnp.concatenate([shard, nothing], axis=0).astype(bf16)
    dinv = dot(dpre, wmix_ref[...], ((1,), (1,)))
    groups = [0, 1, 1, 1, 2, 2, 2, 2, 2]
    for k in range(9):
        part = dinv[:, groups[k] * CHANS : (groups[k] + 1) * CHANS]
        mom_s[k * ATOMS : (k + 1) * ATOMS, :] = (2.0 * msg_scale) * moments[k] * part
    dmom_s[...] = mom_s[...].T.astype(bf16)
    both = jnp.zeros((ROWS + 2 * NB, 2 * CHANS), f32)
    for start in range(0, EDGES, CHUNK):
        at = pl.ds(start, CHUNK)
        dmsg = dot(dmom_s[...], harm_s[:, at], ((1,), (0,)))
        dradial = dmsg * source_s[:, at].astype(f32)
        dsource = (dmsg * radial_s[:, at]).astype(bf16)
        b_top, b_low = split(basis_ref[:, at])
        basis = jnp.concatenate([b_top, b_low], axis=0).astype(bf16)
        left = jnp.concatenate([hot_s[:, at], basis], axis=0)
        right = jnp.concatenate([dsource, dradial.astype(bf16)], axis=0)
        both = both + dot(left, right, ((1,), (1,)))
    dext, gradr = both[:ROWS, :CHANS], both[ROWS:, CHANS:]
    gradr = jnp.concatenate([gradr[:NB] + gradr[NB:], nothing, nothing[:NB]], axis=0)
    send_ref[3 * CHANS // SHARD] = gradr.astype(bf16)
    for i in range(3 * CHANS // SHARD + 1, PEERS):
        send_ref[i] = jnp.zeros((SHARD + GHOST, CHANS), bf16)
    dext_ref[...] = dext[:ATOMS]
    ghosts = [dext[ATOMS + face * GHOST : ATOMS + (face + 1) * GHOST] for face in range(FACES)]
    spot = place()
    for move, block in zip(MOVES, ghosts[:4]):
        to = lax.rem(spot + move + PEERS, PEERS)
        shard = send_ref[to].astype(f32)[:SHARD]
        send_ref[to] = jnp.concatenate([shard, block], axis=0).astype(bf16)
    line_ref[0] = ghosts[4].astype(bf16)
    line_ref[1] = ghosts[5].astype(bf16)


def place():
    return (lax.axis_index("x") * 4 + lax.axis_index("y")) * 2 + lax.axis_index("core")


def passed(got_ref):
    spot = place()
    return [got_ref[lax.rem(spot - move + PEERS, PEERS)].astype(f32)[SHARD:] for move in MOVES]


def add_up(parts_ref, out_ref):
    total = parts_ref[0].astype(f32)[:SHARD]
    for i in range(1, parts_ref.shape[0]):
        total = total + parts_ref[i].astype(f32)[:SHARD]
    total = total.astype(bf16)
    for i in range(out_ref.shape[0]):
        out_ref[i] = total


def slab_kernel(parts_ref, line_ref, out_ref, pass_ref):
    add_up(parts_ref, out_ref)
    blocks = passed(parts_ref)
    odd = lax.rem(lax.axis_index("zl"), 2)
    for i, (down, up) in enumerate([(line_ref[0], line_ref[1]), blocks[:2], blocks[2:]]):
        pass_ref[1 - odd, i] = down.astype(bf16)
        pass_ref[odd, i] = up.astype(bf16)


def line_kernel(parts_ref, p0, p1, out_ref):
    add_up(parts_ref, out_ref)


def feat_kernel(dext_ref, gain_ref, sends_ref, got_ref, p0, p1, dfeat_ref):
    spot = place()
    local = passed(got_ref)
    blocks = []
    a, b = p0[...].astype(f32), p1[...].astype(f32)
    odd = lax.rem(lax.axis_index("zl"), 2)
    down, up = jnp.where(odd == 0, a, b), jnp.where(odd == 0, b, a)
    for move, block, other in zip(MOVES, local, (down[1], up[1], down[2], up[2])):
        crossed = spot - move >= PEERS if move < 0 else spot < move
        blocks.append(jnp.where(crossed, other, block))
    blocks += [down[0], up[0]]
    total = dext_ref[...]
    for face in range(FACES):
        hot = (rows_iota((ATOMS, GHOST)) == sends_ref[face]).astype(f32)
        total = total + dot(hot.astype(bf16), blocks[face].astype(bf16), ((1,), (0,)))
    dfeat_ref[0] = total * gain_ref[...]


def post_kernel(sums_ref, gmix_ref, grad_ref):
    whole = 3 * CHANS // SHARD
    parts = [sums_ref[i].astype(f32) for i in range(whole)]
    grad = sums_ref[whole].astype(f32)[:NB]
    square = grad * grad
    for part in parts:
        for i in range(0, SHARD, NB):
            square = square + part[i : i + NB] * part[i : i + NB]
    norm = jnp.sqrt(jnp.sum(square, keepdims=True))
    factor = clip_norm / jnp.maximum(norm, clip_norm)
    for i, part in enumerate(parts):
        gmix_ref[i * SHARD : (i + 1) * SHARD, :] = factor * part
    grad_ref[...] = factor * grad


def swap(block, parity):
    pairs = []
    for i in range(parity, 128, 2):
        j = (i + 1) % 128
        pairs += [(i, j), (j, i)]
    return lax.ppermute(block, DOM, pairs)


def exchange(blocks, axes):
    return lax.all_to_all(blocks, axes, 0, 0, tiled=True)


def on_device(feat, species, species_gain, send_lists, edge_src, edge_dst, edge_vec, w_rad, w_mix, out_cot):
    shape = jax.ShapeDtypeStruct
    sends = send_lists.reshape(FACES, 1, GHOST)
    own, gain, pair, picks = call(
        pre_kernel,
        [
            shape((ATOMS, CHANS), bf16),
            shape((ATOMS, CHANS), f32),
            shape((2, GHOST, CHANS), bf16),
            shape((RING, GHOST, CHANS), bf16),
        ],
        feat, species, species_gain, sends,
        scratch=[
            pltpu.VMEM((1, ATOMS, CHANS), bf16),
            pltpu.VMEM((1, ATOMS), jnp.int32),
            pltpu.VMEM((5, CHANS), f32),
            pltpu.VMEM((FACES, 1, GHOST), jnp.int32),
            pltpu.SemaphoreType.DMA((4,)),
        ],
        space=pl.ANY,
        limit=60,
    )
    near = [swap(pair[q], q) for q in range(2)]
    far = exchange(picks, PLANE)
    harm, basis = call(
        geo_kernel,
        [shape((16, EDGES), f32), shape((NB, EDGES), f32)],
        edge_vec.reshape(3, 1, EDGES),
        cost=pl.CostEstimate(flops=1000000, bytes_accessed=400000, transcendentals=0),
    )
    dext, line, blocks = call(
        main_kernel,
        [
            shape((ATOMS, CHANS), f32),
            shape((2, GHOST, CHANS), bf16),
            shape((PEERS, SHARD + GHOST, CHANS), bf16),
        ],
        own, *near, far, edge_src, edge_dst, harm, basis, w_rad, w_mix, out_cot,
        scratch=[
            pltpu.VMEM((ROWS, EDGES), bf16),
            pltpu.VMEM((9 * ATOMS, EDGES), bf16),
            pltpu.VMEM((CHANS, EDGES), f32),
            pltpu.VMEM((CHANS, EDGES), bf16),
            pltpu.VMEM((9 * ATOMS, CHANS), f32),
            pltpu.VMEM((CHANS, 9 * ATOMS), bf16),
        ],
    )
    far = exchange(blocks, SLAB)
    parts, passing = call(
        slab_kernel,
        [shape((LINES, SHARD, CHANS), bf16), shape((2, 3, GHOST, CHANS), bf16)],
        far, line,
    )
    pairs = [[(0, 1), (1, 0), (2, 3), (3, 2)], [(1, 2), (2, 1), (3, 0), (0, 3)]]
    passing = [lax.ppermute(passing[q], "zl", pairs[q]) for q in range(2)]
    parts = exchange(parts, LINE)
    (parts,) = call(line_kernel, [shape((PEERS, SHARD, CHANS), bf16)], parts, *passing)
    sums = exchange(parts, SLAB)
    (d_feat,) = call(
        feat_kernel,
        [shape((1, ATOMS, CHANS), f32)],
        dext, gain, sends, far, *passing,
        cost=pl.CostEstimate(flops=10000000, bytes_accessed=500000, transcendentals=0),
    )
    gmix, grad_r = call(
        post_kernel, [shape((3 * CHANS, CHANS), f32), shape((NB, CHANS), f32)], sums
    )
    return d_feat, gmix, grad_r


def solution(mesh):
    fine = Mesh(mesh.devices.reshape(4, 4, 4, 2, 4), DOM + ("rep",))
    in_specs = (
        P("rep", DOM, None),
        P("rep", DOM),
        P(),
        P("rep", None, DOM),
        P("rep", DOM),
        P("rep", DOM),
        P("rep", None, DOM),
        P(),
        P(),
        P("rep", DOM, None),
    )
    out_specs = (P("rep", DOM, None), P(), P())
    return jax.shard_map(
        on_device, mesh=fine, in_specs=in_specs, out_specs=out_specs, check_vma=False
    )
```

```python
import jax
import jax.numpy as jnp
import numpy as np
from jax import lax
from jax.experimental import pallas as pl
from jax.experimental.pallas import tpu as pltpu
from jax.sharding import Mesh, PartitionSpec as P

msg_scale = 0.35
cutoff = 6.0
clip_norm = 256.0
f32, bf16 = jnp.float32, jnp.bfloat16

CHANS = 128
NB = 8
ATOMS = 64
FACES = 6
GHOST = 24
ROWS = ATOMS + FACES * GHOST
EDGES = 4096
CHUNK = 1024
SHARD = 16
RING = 16
PLANE = ("zl", "x")
PEERS = 32
SLAB = ("x", "y", "core")
LINE = ("zl", "rep")
LINES = 16
MOVES = (-1, 1, -8, 8)
DOM = ("zl", "x", "y", "core")
STRIDES = (1, -1, 4, -4)


def dot(a, b, dims):
    return lax.dot_general(a, b, (dims, ((), ())), preferred_element_type=f32)


def rows_iota(shape):
    return lax.broadcasted_iota(jnp.int32, shape, 0)


def call(kernel, outs, *args, scratch=(), cost=None, space=pltpu.VMEM, limit=48):
    return pl.pallas_call(
        kernel,
        out_shape=outs,
        in_specs=[pl.BlockSpec(memory_space=space) for _ in args],
        out_specs=[pl.BlockSpec(memory_space=pltpu.VMEM) for _ in outs],
        scratch_shapes=list(scratch),
        cost_estimate=cost,
        compiler_params=pltpu.CompilerParams(vmem_limit_bytes=limit * 1024 * 1024),
    )(*args)


def position():
    ring = lax.axis_index("zl") * 4 + lax.axis_index("x")
    return ring, lax.axis_index("core")


def peer(ring, stride):
    return lax.rem(ring + stride + RING, RING)


def pre_kernel(
    feat_hbm, species_hbm, gain_hbm, sends_hbm, own_ref, gain_out, pair_ref, pick_ref,
    feat_ref, species_ref, gain_ref, sends_ref, sems,
):
    copies = [
        pltpu.make_async_copy(src, dst, sems.at[i])
        for i, (src, dst) in enumerate(
            [
                (feat_hbm, feat_ref),
                (species_hbm, species_ref),
                (gain_hbm, gain_ref),
                (sends_hbm, sends_ref),
            ]
        )
    ]
    for copy in copies:
        copy.start()
    pick_ref[...] = jnp.zeros_like(pick_ref)
    for copy in copies:
        copy.wait()
    hot = (rows_iota((8, ATOMS)) == species_ref[...]).astype(f32)
    gains = jnp.concatenate([gain_ref[...], jnp.zeros((3, CHANS), f32)], axis=0)
    top, low = split(gains)
    gains = jnp.concatenate([top, *split(low)], axis=0).astype(bf16)
    gain = dot(jnp.concatenate([hot] * 3, axis=0).astype(bf16), gains, ((0,), (0,)))
    own = (feat_ref[0].astype(f32) * gain).astype(bf16)
    own_ref[...] = own
    gain_out[...] = gain
    ring, core = position()
    for face in range(FACES):
        hot = (rows_iota((ATOMS, GHOST)) == sends_ref[face]).astype(f32)
        picked = dot(hot.astype(bf16), own, ((0,), (0,))).astype(bf16)
        if face < 2:
            pair_ref[lax.rem(core + face, 2)] = picked
        else:
            pick_ref[peer(ring, STRIDES[face - 2])] = picked


def geo_kernel(vec_ref, harm_ref, basis_ref):
    vx, vy, vz = (vec_ref[i] for i in range(3))
    square = vx * vx + vy * vy + vz * vz + 0.25
    inv_r = lax.rsqrt(square)
    radius = square * inv_r
    ux, uy, uz = vx * inv_r, vy * inv_r, vz * inv_r
    r3, r5, r15 = 3.0**0.5, 5.0**0.5, 15.0**0.5
    harms = [
        jnp.ones_like(ux),
        r3 * ux,
        r3 * uy,
        r3 * uz,
        r15 * ux * uy,
        r15 * uy * uz,
        0.5 * r5 * (3.0 * uz * uz - 1.0),
        r15 * ux * uz,
        0.5 * r15 * (ux * ux - uy * uy),
    ]
    for k, h in enumerate(harms):
        harm_ref[k : k + 1, :] = h
    scaled = radius * (1.0 / cutoff)
    envelope = 1.0 - scaled * scaled
    envelope = envelope * envelope * inv_r
    t = scaled * np.float32(np.pi) - np.float32(np.pi / 2)
    t2 = t * t
    sin_t = series(t2, 1) * t
    cos_t = series(t2, 0)
    twice = -2.0 * sin_t
    before, now = jnp.zeros_like(t), cos_t * envelope
    for b in range(NB):
        basis_ref[b : b + 1, :] = now
        before, now = now, twice * now - before


def series(square, odd):
    terms = [(-1.0) ** n / float(np.prod(np.arange(1, 2 * n + odd + 1.0))) for n in range(9)]
    total = jnp.full_like(square, terms[-1])
    for term in terms[-2::-1]:
        total = total * square + term
    return total


def split(values):
    top = values.astype(bf16).astype(f32)
    return top, values - top


def main_kernel(
    own_ref, p0, p1, got_ref, src_ref, dst_ref, harm_ref, basis_ref, wrad_ref, wmix_ref, cot_ref,
    dext_ref, line_ref, send_ref,
    hot_s, harm_s, radial_s, source_s, mom_s, dmom_s,
):
    ring, core = position()
    a, b = p0[...].astype(f32), p1[...].astype(f32)
    blocks = [own_ref[...].astype(f32), jnp.where(core == 0, b, a), jnp.where(core == 0, a, b)]
    for stride in STRIDES:
        blocks.append(got_ref[peer(ring, -stride)].astype(f32))
    ext = jnp.concatenate(blocks, axis=0).T.astype(bf16)
    w_top, w_low = split(wrad_ref[...])
    wrad = jnp.concatenate([w_top, w_low, w_top], axis=0).T.astype(bf16)
    turned = jnp.zeros((CHANS, 9 * ATOMS), f32)
    for start in range(0, EDGES, CHUNK):
        at = pl.ds(start, CHUNK)
        src = src_ref[:, at]
        hot = jnp.where(rows_iota((ROWS, CHUNK)) == src, 1.0, 0.0).astype(bf16)
        hot_s[:, at] = hot
        source = dot(ext, hot, ((1,), (0,)))
        source_s[:, at] = source.astype(bf16)
        b_top, b_low = split(basis_ref[:, at])
        basis = jnp.concatenate([b_top, b_top, b_low], axis=0).astype(bf16)
        radial = dot(wrad, basis, ((1,), (0,)))
        radial_s[:, at] = radial
        message = (radial * source).astype(bf16)
        own_hot = rows_iota((ATOMS, CHUNK)) == dst_ref[:, at]
        own_hot = jnp.where(own_hot, 1.0, 0.0).astype(bf16)
        harm_s[0:ATOMS, at] = own_hot
        for k in range(1, 9):
            harm = harm_ref[k : k + 1, at]
            harm_s[k * ATOMS : (k + 1) * ATOMS, at] = own_hot * harm.astype(bf16)
        turned = turned + dot(message, harm_s[:, at], ((1,), (1,)))
    mom_s[...] = turned.T
    moments = [msg_scale * mom_s[k * ATOMS : (k + 1) * ATOMS, :] for k in range(9)]
    squares = [m * m for m in moments]
    two = squares[4]
    for k in range(5, 9):
        two = two + squares[k]
    inv = jnp.concatenate([squares[0], squares[1] + squares[2] + squares[3], two], axis=1).astype(bf16)
    pre = dot(inv, wmix_ref[...], ((1,), (0,)))
    sigma = jax.nn.sigmoid(pre)
    slope = sigma * (1.0 + pre * (1.0 - sigma))
    dpre = (cot_ref[0].astype(f32) * slope).astype(bf16)
    gmix = dot(inv, dpre, ((0,), (0,)))
    nothing = jnp.zeros((GHOST, CHANS), f32)
    for i in range(3 * CHANS // SHARD):
        shard = gmix[i * SHARD : (i + 1) * SHARD]
        send_ref[i] = jnp.concatenate([shard, nothing], axis=0).astype(bf16)
    dinv = dot(dpre, wmix_ref[...], ((1,), (1,)))
    groups = [0, 1, 1, 1, 2, 2, 2, 2, 2]
    for k in range(9):
        part = dinv[:, groups[k] * CHANS : (groups[k] + 1) * CHANS]
        mom_s[k * ATOMS : (k + 1) * ATOMS, :] = (2.0 * msg_scale) * moments[k] * part
    dmom_s[...] = mom_s[...].T.astype(bf16)
    both = jnp.zeros((ROWS + 2 * NB, 2 * CHANS), f32)
    for start in range(0, EDGES, CHUNK):
        at = pl.ds(start, CHUNK)
        dmsg = dot(dmom_s[...], harm_s[:, at], ((1,), (0,)))
        dradial = dmsg * source_s[:, at].astype(f32)
        dsource = (dmsg * radial_s[:, at]).astype(bf16)
        b_top, b_low = split(basis_ref[:, at])
        basis = jnp.concatenate([b_top, b_low], axis=0).astype(bf16)
        left = jnp.concatenate([hot_s[:, at], basis], axis=0)
        right = jnp.concatenate([dsource, dradial.astype(bf16)], axis=0)
        both = both + dot(left, right, ((1,), (1,)))
    dext, gradr = both[:ROWS, :CHANS], both[ROWS:, CHANS:]
    gradr = jnp.concatenate([gradr[:NB] + gradr[NB:], nothing, nothing[:NB]], axis=0)
    send_ref[3 * CHANS // SHARD] = gradr.astype(bf16)
    for i in range(3 * CHANS // SHARD + 1, PEERS):
        send_ref[i] = jnp.zeros((SHARD + GHOST, CHANS), bf16)
    dext_ref[...] = dext[:ATOMS]
    ghosts = [dext[ATOMS + face * GHOST : ATOMS + (face + 1) * GHOST] for face in range(FACES)]
    spot = place()
    for move, block in zip(MOVES, ghosts[:4]):
        to = lax.rem(spot + move + PEERS, PEERS)
        shard = send_ref[to].astype(f32)[:SHARD]
        send_ref[to] = jnp.concatenate([shard, block], axis=0).astype(bf16)
    line_ref[0] = ghosts[4].astype(bf16)
    line_ref[1] = ghosts[5].astype(bf16)


def place():
    return (lax.axis_index("x") * 4 + lax.axis_index("y")) * 2 + lax.axis_index("core")


def passed(got_ref):
    spot = place()
    return [got_ref[lax.rem(spot - move + PEERS, PEERS)].astype(f32)[SHARD:] for move in MOVES]


def add_up(parts_ref, out_ref):
    total = parts_ref[0].astype(f32)[:SHARD]
    for i in range(1, parts_ref.shape[0]):
        total = total + parts_ref[i].astype(f32)[:SHARD]
    total = total.astype(bf16)
    for i in range(out_ref.shape[0]):
        out_ref[i] = total


def slab_kernel(parts_ref, line_ref, out_ref, pass_ref):
    add_up(parts_ref, out_ref)
    blocks = passed(parts_ref)
    odd = lax.rem(lax.axis_index("zl"), 2)
    for i, (down, up) in enumerate([(line_ref[0], line_ref[1]), blocks[:2], blocks[2:]]):
        pass_ref[1 - odd, i] = down.astype(bf16)
        pass_ref[odd, i] = up.astype(bf16)


def line_kernel(parts_ref, p0, p1, out_ref):
    add_up(parts_ref, out_ref)


def post_kernel(
    dext_ref, gain_ref, sends_ref, got_ref, p0, p1, sums_ref, dfeat_ref, gmix_ref, grad_ref
):
    spot = place()
    local = passed(got_ref)
    blocks = []
    a, b = p0[...].astype(f32), p1[...].astype(f32)
    odd = lax.rem(lax.axis_index("zl"), 2)
    down, up = jnp.where(odd == 0, a, b), jnp.where(odd == 0, b, a)
    for move, block, other in zip(MOVES, local, (down[1], up[1], down[2], up[2])):
        crossed = spot - move >= PEERS if move < 0 else spot < move
        blocks.append(jnp.where(crossed, other, block))
    blocks += [down[0], up[0]]
    total = dext_ref[...]
    for face in range(FACES):
        hot = (rows_iota((ATOMS, GHOST)) == sends_ref[face]).astype(f32)
        total = total + dot(hot.astype(bf16), blocks[face].astype(bf16), ((1,), (0,)))
    dfeat_ref[0] = total * gain_ref[...]
    whole = 3 * CHANS // SHARD
    parts = [sums_ref[i].astype(f32) for i in range(whole)]
    grad = sums_ref[whole].astype(f32)[:NB]
    square = grad * grad
    for part in parts:
        for i in range(0, SHARD, NB):
            square = square + part[i : i + NB] * part[i : i + NB]
    norm = jnp.sqrt(jnp.sum(square, keepdims=True))
    factor = clip_norm / jnp.maximum(norm, clip_norm)
    for i, part in enumerate(parts):
        gmix_ref[i * SHARD : (i + 1) * SHARD, :] = factor * part
    grad_ref[...] = factor * grad


def swap(block, parity):
    pairs = []
    for i in range(parity, 128, 2):
        j = (i + 1) % 128
        pairs += [(i, j), (j, i)]
    return lax.ppermute(block, DOM, pairs)


def exchange(blocks, axes):
    return lax.all_to_all(blocks, axes, 0, 0, tiled=True)


def on_device(feat, species, species_gain, send_lists, edge_src, edge_dst, edge_vec, w_rad, w_mix, out_cot):
    shape = jax.ShapeDtypeStruct
    sends = send_lists.reshape(FACES, 1, GHOST)
    own, gain, pair, picks = call(
        pre_kernel,
        [
            shape((ATOMS, CHANS), bf16),
            shape((ATOMS, CHANS), f32),
            shape((2, GHOST, CHANS), bf16),
            shape((RING, GHOST, CHANS), bf16),
        ],
        feat, species, species_gain, sends,
        scratch=[
            pltpu.VMEM((1, ATOMS, CHANS), bf16),
            pltpu.VMEM((1, ATOMS), jnp.int32),
            pltpu.VMEM((5, CHANS), f32),
            pltpu.VMEM((FACES, 1, GHOST), jnp.int32),
            pltpu.SemaphoreType.DMA((4,)),
        ],
        space=pl.ANY,
        limit=60,
    )
    near = [swap(pair[q], q) for q in range(2)]
    far = exchange(picks, PLANE)
    harm, basis = call(
        geo_kernel,
        [shape((16, EDGES), f32), shape((NB, EDGES), f32)],
        edge_vec.reshape(3, 1, EDGES),
        cost=pl.CostEstimate(flops=1000000, bytes_accessed=400000, transcendentals=0),
    )
    dext, line, blocks = call(
        main_kernel,
        [
            shape((ATOMS, CHANS), f32),
            shape((2, GHOST, CHANS), bf16),
            shape((PEERS, SHARD + GHOST, CHANS), bf16),
        ],
        own, *near, far, edge_src, edge_dst, harm, basis, w_rad, w_mix, out_cot,
        scratch=[
            pltpu.VMEM((ROWS, EDGES), bf16),
            pltpu.VMEM((9 * ATOMS, EDGES), bf16),
            pltpu.VMEM((CHANS, EDGES), f32),
            pltpu.VMEM((CHANS, EDGES), bf16),
            pltpu.VMEM((9 * ATOMS, CHANS), f32),
            pltpu.VMEM((CHANS, 9 * ATOMS), bf16),
        ],
    )
    far = exchange(blocks, SLAB)
    parts, passing = call(
        slab_kernel,
        [shape((LINES, SHARD, CHANS), bf16), shape((2, 3, GHOST, CHANS), bf16)],
        far, line,
    )
    pairs = [[(0, 1), (1, 0), (2, 3), (3, 2)], [(1, 2), (2, 1), (3, 0), (0, 3)]]
    passing = [lax.ppermute(passing[q], "zl", pairs[q]) for q in range(2)]
    parts = exchange(parts, LINE)
    (parts,) = call(line_kernel, [shape((PEERS, SHARD, CHANS), bf16)], parts, *passing)
    sums = exchange(parts, SLAB)
    d_feat, gmix, grad_r = call(
        post_kernel,
        [shape((1, ATOMS, CHANS), f32), shape((3 * CHANS, CHANS), f32), shape((NB, CHANS), f32)],
        dext, gain, sends, far, *passing, sums,
    )
    return d_feat, gmix, grad_r


def solution(mesh):
    fine = Mesh(mesh.devices.reshape(4, 4, 4, 2, 4), DOM + ("rep",))
    in_specs = (
        P("rep", DOM, None),
        P("rep", DOM),
        P(),
        P("rep", None, DOM),
        P("rep", DOM),
        P("rep", DOM),
        P("rep", None, DOM),
        P(),
        P(),
        P("rep", DOM, None),
    )
    out_specs = (P("rep", DOM, None), P(), P())
    return jax.shard_map(
        on_device, mesh=fine, in_specs=in_specs, out_specs=out_specs, check_vma=False
    )
```

```python
import jax
import jax.numpy as jnp
import numpy as np
from jax import lax
from jax.experimental import pallas as pl
from jax.experimental.pallas import tpu as pltpu
from jax.sharding import Mesh, PartitionSpec as P

msg_scale = 0.35
cutoff = 6.0
clip_norm = 256.0
f32, bf16 = jnp.float32, jnp.bfloat16

CHANS = 128
NB = 8
ATOMS = 64
FACES = 6
GHOST = 24
ROWS = ATOMS + FACES * GHOST
EDGES = 4096
CHUNK = 1024
SHARD = 16
RING = 16
PLANE = ("zl", "x")
PEERS = 32
SLAB = ("x", "y", "core")
LINE = ("zl", "rep")
LINES = 16
MOVES = (-1, 1, -8, 8)
DOM = ("zl", "x", "y", "core")
STRIDES = (1, -1, 4, -4)


def dot(a, b, dims):
    return lax.dot_general(a, b, (dims, ((), ())), preferred_element_type=f32)


def rows_iota(shape):
    return lax.broadcasted_iota(jnp.int32, shape, 0)


def call(kernel, outs, *args, scratch=(), cost=None, space=pltpu.VMEM, limit=48):
    return pl.pallas_call(
        kernel,
        out_shape=outs,
        in_specs=[pl.BlockSpec(memory_space=space) for _ in args],
        out_specs=[pl.BlockSpec(memory_space=pltpu.VMEM) for _ in outs],
        scratch_shapes=list(scratch),
        cost_estimate=cost,
        compiler_params=pltpu.CompilerParams(vmem_limit_bytes=limit * 1024 * 1024),
    )(*args)


def position():
    ring = lax.axis_index("zl") * 4 + lax.axis_index("x")
    return ring, lax.axis_index("core")


def peer(ring, stride):
    return lax.rem(ring + stride + RING, RING)


def pre_kernel(
    feat_hbm, species_hbm, gain_hbm, sends_hbm, own_ref, gain_out, pair_ref, pick_ref,
    feat_ref, species_ref, gain_ref, sends_ref, sems,
):
    copies = [
        pltpu.make_async_copy(src, dst, sems.at[i])
        for i, (src, dst) in enumerate(
            [
                (feat_hbm, feat_ref),
                (species_hbm, species_ref),
                (gain_hbm, gain_ref),
                (sends_hbm, sends_ref),
            ]
        )
    ]
    for copy in copies:
        copy.start()
    pick_ref[...] = jnp.zeros_like(pick_ref)
    for copy in copies:
        copy.wait()
    hot = (rows_iota((8, ATOMS)) == species_ref[...]).astype(f32)
    gains = jnp.concatenate([gain_ref[...], jnp.zeros((3, CHANS), f32)], axis=0)
    top, low = split(gains)
    gains = jnp.concatenate([top, *split(low)], axis=0).astype(bf16)
    gain = dot(jnp.concatenate([hot] * 3, axis=0).astype(bf16), gains, ((0,), (0,)))
    own = (feat_ref[0].astype(f32) * gain).astype(bf16)
    own_ref[...] = own
    gain_out[...] = gain
    ring, core = position()
    for face in range(FACES):
        hot = (rows_iota((ATOMS, GHOST)) == sends_ref[face]).astype(f32)
        picked = dot(hot.astype(bf16), own, ((0,), (0,))).astype(bf16)
        if face < 2:
            pair_ref[lax.rem(core + face, 2)] = picked
        else:
            pick_ref[peer(ring, STRIDES[face - 2])] = picked


def geo_kernel(vec_ref, harm_ref, basis_ref):
    vx, vy, vz = (vec_ref[i] for i in range(3))
    square = vx * vx + vy * vy + vz * vz + 0.25
    inv_r = lax.rsqrt(square)
    radius = square * inv_r
    ux, uy, uz = vx * inv_r, vy * inv_r, vz * inv_r
    r3, r5, r15 = 3.0**0.5, 5.0**0.5, 15.0**0.5
    harms = [
        jnp.ones_like(ux),
        r3 * ux,
        r3 * uy,
        r3 * uz,
        r15 * ux * uy,
        r15 * uy * uz,
        0.5 * r5 * (3.0 * uz * uz - 1.0),
        r15 * ux * uz,
        0.5 * r15 * (ux * ux - uy * uy),
    ]
    for k, h in enumerate(harms):
        harm_ref[k : k + 1, :] = h
    scaled = radius * (1.0 / cutoff)
    envelope = 1.0 - scaled * scaled
    envelope = envelope * envelope * inv_r
    t = scaled * np.float32(np.pi) - np.float32(np.pi / 2)
    t2 = t * t
    sin_t = series(t2, 1) * t
    cos_t = series(t2, 0)
    twice = -2.0 * sin_t
    before, now = jnp.zeros_like(t), cos_t * envelope
    for b in range(NB):
        basis_ref[b : b + 1, :] = now
        before, now = now, twice * now - before


def series(square, odd):
    terms = [(-1.0) ** n / float(np.prod(np.arange(1, 2 * n + odd + 1.0))) for n in range(9)]
    total = jnp.full_like(square, terms[-1])
    for term in terms[-2::-1]:
        total = total * square + term
    return total


def split(values):
    top = values.astype(bf16).astype(f32)
    return top, values - top


def main_kernel(
    own_ref, p0, p1, got_ref, src_ref, dst_ref, harm_ref, basis_ref, wrad_ref, wmix_ref, cot_ref,
    lists_ref, dext_ref, line_ref, send_ref, lists_out,
    hot_s, harm_s, radial_s, source_s, mom_s, dmom_s,
):
    ring, core = position()
    a, b = p0[...].astype(f32), p1[...].astype(f32)
    blocks = [own_ref[...].astype(f32), jnp.where(core == 0, b, a), jnp.where(core == 0, a, b)]
    for stride in STRIDES:
        blocks.append(got_ref[peer(ring, -stride)].astype(f32))
    ext = jnp.concatenate(blocks, axis=0).T.astype(bf16)
    w_top, w_low = split(wrad_ref[...])
    wrad = jnp.concatenate([w_top, w_low, w_top], axis=0).T.astype(bf16)
    turned = jnp.zeros((CHANS, 9 * ATOMS), f32)
    for start in range(0, EDGES, CHUNK):
        at = pl.ds(start, CHUNK)
        src = src_ref[:, at]
        hot = jnp.where(rows_iota((ROWS, CHUNK)) == src, 1.0, 0.0).astype(bf16)
        hot_s[:, at] = hot
        source = dot(ext, hot, ((1,), (0,)))
        source_s[:, at] = source.astype(bf16)
        b_top, b_low = split(basis_ref[:, at])
        basis = jnp.concatenate([b_top, b_top, b_low], axis=0).astype(bf16)
        radial = dot(wrad, basis, ((1,), (0,)))
        radial_s[:, at] = radial
        message = (radial * source).astype(bf16)
        own_hot = rows_iota((ATOMS, CHUNK)) == dst_ref[:, at]
        own_hot = jnp.where(own_hot, 1.0, 0.0).astype(bf16)
        harm_s[0:ATOMS, at] = own_hot
        for k in range(1, 9):
            harm = harm_ref[k : k + 1, at]
            harm_s[k * ATOMS : (k + 1) * ATOMS, at] = own_hot * harm.astype(bf16)
        turned = turned + dot(message, harm_s[:, at], ((1,), (1,)))
    mom_s[...] = turned.T
    moments = [msg_scale * mom_s[k * ATOMS : (k + 1) * ATOMS, :] for k in range(9)]
    squares = [m * m for m in moments]
    two = squares[4]
    for k in range(5, 9):
        two = two + squares[k]
    inv = jnp.concatenate([squares[0], squares[1] + squares[2] + squares[3], two], axis=1).astype(bf16)
    pre = dot(inv, wmix_ref[...], ((1,), (0,)))
    sigma = jax.nn.sigmoid(pre)
    slope = sigma * (1.0 + pre * (1.0 - sigma))
    dpre = (cot_ref[0].astype(f32) * slope).astype(bf16)
    gmix = dot(inv, dpre, ((0,), (0,)))
    nothing = jnp.zeros((GHOST, CHANS), f32)
    for i in range(3 * CHANS // SHARD):
        shard = gmix[i * SHARD : (i + 1) * SHARD]
        send_ref[i] = jnp.concatenate([shard, nothing], axis=0).astype(bf16)
    dinv = dot(dpre, wmix_ref[...], ((1,), (1,)))
    groups = [0, 1, 1, 1, 2, 2, 2, 2, 2]
    for k in range(9):
        part = dinv[:, groups[k] * CHANS : (groups[k] + 1) * CHANS]
        mom_s[k * ATOMS : (k + 1) * ATOMS, :] = (2.0 * msg_scale) * moments[k] * part
    dmom_s[...] = mom_s[...].T.astype(bf16)
    both = jnp.zeros((ROWS + 2 * NB, 2 * CHANS), f32)
    for start in range(0, EDGES, CHUNK):
        at = pl.ds(start, CHUNK)
        dmsg = dot(dmom_s[...], harm_s[:, at], ((1,), (0,)))
        dradial = dmsg * source_s[:, at].astype(f32)
        dsource = (dmsg * radial_s[:, at]).astype(bf16)
        b_top, b_low = split(basis_ref[:, at])
        basis = jnp.concatenate([b_top, b_low], axis=0).astype(bf16)
        left = jnp.concatenate([hot_s[:, at], basis], axis=0)
        right = jnp.concatenate([dsource, dradial.astype(bf16)], axis=0)
        both = both + dot(left, right, ((1,), (1,)))
    dext, gradr = both[:ROWS, :CHANS], both[ROWS:, CHANS:]
    gradr = jnp.concatenate([gradr[:NB] + gradr[NB:], nothing, nothing[:NB]], axis=0)
    send_ref[3 * CHANS // SHARD] = gradr.astype(bf16)
    for i in range(3 * CHANS // SHARD + 1, PEERS):
        send_ref[i] = jnp.zeros((SHARD + GHOST, CHANS), bf16)
    dext_ref[...] = dext[:ATOMS]
    ghosts = [dext[ATOMS + face * GHOST : ATOMS + (face + 1) * GHOST] for face in range(FACES)]
    spot = place()
    for move, block in zip(MOVES, ghosts[:4]):
        to = lax.rem(spot + move + PEERS, PEERS)
        shard = send_ref[to].astype(f32)[:SHARD]
        send_ref[to] = jnp.concatenate([shard, block], axis=0).astype(bf16)
    line_ref[0] = ghosts[4].astype(bf16)
    line_ref[1] = ghosts[5].astype(bf16)
    lists_out[...] = lists_ref[...]


def place():
    return (lax.axis_index("x") * 4 + lax.axis_index("y")) * 2 + lax.axis_index("core")


def passed(got_ref):
    spot = place()
    return [got_ref[lax.rem(spot - move + PEERS, PEERS)].astype(f32)[SHARD:] for move in MOVES]


def add_up(parts_ref, out_ref):
    total = parts_ref[0].astype(f32)[:SHARD]
    for i in range(1, parts_ref.shape[0]):
        total = total + parts_ref[i].astype(f32)[:SHARD]
    total = total.astype(bf16)
    for i in range(out_ref.shape[0]):
        out_ref[i] = total


def slab_kernel(parts_ref, line_ref, out_ref, pass_ref):
    add_up(parts_ref, out_ref)
    blocks = passed(parts_ref)
    level = lax.axis_index("zl")
    pass_ref[...] = jnp.zeros_like(pass_ref)
    for i, (down, up) in enumerate([(line_ref[0], line_ref[1]), blocks[:2], blocks[2:]]):
        pass_ref[lax.rem(level + 3, 4), i] = down.astype(bf16)
        pass_ref[lax.rem(level + 1, 4), i] = up.astype(bf16)


def line_kernel(parts_ref, passed_ref, out_ref):
    add_up(parts_ref, out_ref)


def post_kernel(
    dext_ref, gain_ref, sends_ref, got_ref, passed_ref, sums_ref, dfeat_ref, gmix_ref, grad_ref
):
    spot = place()
    local = passed(got_ref)
    blocks = []
    level = lax.axis_index("zl")
    down = passed_ref[lax.rem(level + 1, 4)].astype(f32)
    up = passed_ref[lax.rem(level + 3, 4)].astype(f32)
    for move, block, other in zip(MOVES, local, (down[1], up[1], down[2], up[2])):
        crossed = spot - move >= PEERS if move < 0 else spot < move
        blocks.append(jnp.where(crossed, other, block))
    blocks += [down[0], up[0]]
    total = dext_ref[...]
    for face in range(FACES):
        hot = (rows_iota((ATOMS, GHOST)) == sends_ref[face]).astype(f32)
        total = total + dot(hot.astype(bf16), blocks[face].astype(bf16), ((1,), (0,)))
    dfeat_ref[0] = total * gain_ref[...]
    whole = 3 * CHANS // SHARD
    parts = [sums_ref[i].astype(f32) for i in range(whole)]
    grad = sums_ref[whole].astype(f32)[:NB]
    square = grad * grad
    for part in parts:
        for i in range(0, SHARD, NB):
            square = square + part[i : i + NB] * part[i : i + NB]
    norm = jnp.sqrt(jnp.sum(square, keepdims=True))
    factor = clip_norm / jnp.maximum(norm, clip_norm)
    for i, part in enumerate(parts):
        gmix_ref[i * SHARD : (i + 1) * SHARD, :] = factor * part
    grad_ref[...] = factor * grad


def swap(block, parity):
    pairs = []
    for i in range(parity, 128, 2):
        j = (i + 1) % 128
        pairs += [(i, j), (j, i)]
    return lax.ppermute(block, DOM, pairs)


def exchange(blocks, axes):
    return lax.all_to_all(blocks, axes, 0, 0, tiled=True)


def on_device(feat, species, species_gain, send_lists, edge_src, edge_dst, edge_vec, w_rad, w_mix, out_cot):
    shape = jax.ShapeDtypeStruct
    sends = send_lists.reshape(FACES, 1, GHOST)
    own, gain, pair, picks = call(
        pre_kernel,
        [
            shape((ATOMS, CHANS), bf16),
            shape((ATOMS, CHANS), f32),
            shape((2, GHOST, CHANS), bf16),
            shape((RING, GHOST, CHANS), bf16),
        ],
        feat, species, species_gain, sends,
        scratch=[
            pltpu.VMEM((1, ATOMS, CHANS), bf16),
            pltpu.VMEM((1, ATOMS), jnp.int32),
            pltpu.VMEM((5, CHANS), f32),
            pltpu.VMEM((FACES, 1, GHOST), jnp.int32),
            pltpu.SemaphoreType.DMA((4,)),
        ],
        space=pl.ANY,
        limit=60,
    )
    near = [swap(pair[q], q) for q in range(2)]
    far = exchange(picks, PLANE)
    harm, basis = call(
        geo_kernel,
        [shape((16, EDGES), f32), shape((NB, EDGES), f32)],
        edge_vec.reshape(3, 1, EDGES),
        cost=pl.CostEstimate(flops=1000000, bytes_accessed=400000, transcendentals=0),
    )
    dext, line, blocks, lists = call(
        main_kernel,
        [
            shape((ATOMS, CHANS), f32),
            shape((2, GHOST, CHANS), bf16),
            shape((PEERS, SHARD + GHOST, CHANS), bf16),
            shape((FACES, 1, GHOST), jnp.int32),
        ],
        own, *near, far, edge_src, edge_dst, harm, basis, w_rad, w_mix, out_cot, sends,
        scratch=[
            pltpu.VMEM((ROWS, EDGES), bf16),
            pltpu.VMEM((9 * ATOMS, EDGES), bf16),
            pltpu.VMEM((CHANS, EDGES), f32),
            pltpu.VMEM((CHANS, EDGES), bf16),
            pltpu.VMEM((9 * ATOMS, CHANS), f32),
            pltpu.VMEM((CHANS, 9 * ATOMS), bf16),
        ],
    )
    far = exchange(blocks, SLAB)
    parts, passing = call(
        slab_kernel,
        [shape((LINES, SHARD, CHANS), bf16), shape((4, 3, GHOST, CHANS), bf16)],
        far, line,
    )
    passing = exchange(passing, "zl")
    parts = exchange(parts, LINE)
    (parts,) = call(line_kernel, [shape((PEERS, SHARD, CHANS), bf16)], parts, passing)
    sums = exchange(parts, SLAB)
    d_feat, gmix, grad_r = call(
        post_kernel,
        [shape((1, ATOMS, CHANS), f32), shape((3 * CHANS, CHANS), f32), shape((NB, CHANS), f32)],
        dext, gain, lists, far, passing, sums,
    )
    return d_feat, gmix, grad_r


def solution(mesh):
    fine = Mesh(mesh.devices.reshape(4, 4, 4, 2, 4), DOM + ("rep",))
    in_specs = (
        P("rep", DOM, None),
        P("rep", DOM),
        P(),
        P("rep", None, DOM),
        P("rep", DOM),
        P("rep", DOM),
        P("rep", None, DOM),
        P(),
        P(),
        P("rep", DOM, None),
    )
    out_specs = (P("rep", DOM, None), P(), P())
    return jax.shard_map(
        on_device, mesh=fine, in_specs=in_specs, out_specs=out_specs, check_vma=False
    )
```

```python
import jax
import jax.numpy as jnp
import numpy as np
from jax import lax
from jax.experimental import pallas as pl
from jax.experimental.pallas import tpu as pltpu
from jax.sharding import Mesh, PartitionSpec as P

msg_scale = 0.35
cutoff = 6.0
clip_norm = 256.0
f32, bf16 = jnp.float32, jnp.bfloat16

CHANS = 128
NB = 8
ATOMS = 64
FACES = 6
GHOST = 24
ROWS = ATOMS + FACES * GHOST
EDGES = 4096
CHUNK = 1024
SHARD = 16
RING = 16
PLANE = ("zl", "x")
PEERS = 32
SLAB = ("x", "y", "core")
LINE = ("zl", "rep")
LINES = 16
MOVES = (-1, 1, -8, 8)
DOM = ("zl", "x", "y", "core")
STRIDES = (1, -1, 4, -4)


def dot(a, b, dims):
    return lax.dot_general(a, b, (dims, ((), ())), preferred_element_type=f32)


def rows_iota(shape):
    return lax.broadcasted_iota(jnp.int32, shape, 0)


def call(kernel, outs, *args, scratch=(), cost=None, space=pltpu.VMEM, limit=48):
    return pl.pallas_call(
        kernel,
        out_shape=outs,
        in_specs=[pl.BlockSpec(memory_space=space) for _ in args],
        out_specs=[pl.BlockSpec(memory_space=pltpu.VMEM) for _ in outs],
        scratch_shapes=list(scratch),
        cost_estimate=cost,
        compiler_params=pltpu.CompilerParams(vmem_limit_bytes=limit * 1024 * 1024),
    )(*args)


def position():
    ring = lax.axis_index("zl") * 4 + lax.axis_index("x")
    return ring, lax.axis_index("core")


def peer(ring, stride):
    return lax.rem(ring + stride + RING, RING)


def pre_kernel(
    feat_hbm, species_hbm, gain_hbm, sends_hbm, own_ref, gain_out, pair_ref, pick_ref,
    feat_ref, species_ref, gain_ref, sends_ref, sems,
):
    copies = [
        pltpu.make_async_copy(src, dst, sems.at[i])
        for i, (src, dst) in enumerate(
            [
                (feat_hbm, feat_ref),
                (species_hbm, species_ref),
                (gain_hbm, gain_ref),
                (sends_hbm, sends_ref),
            ]
        )
    ]
    for copy in copies:
        copy.start()
    pick_ref[...] = jnp.zeros_like(pick_ref)
    for copy in copies:
        copy.wait()
    hot = (rows_iota((8, ATOMS)) == species_ref[...]).astype(f32)
    gains = jnp.concatenate([gain_ref[...], jnp.zeros((3, CHANS), f32)], axis=0)
    top, low = split(gains)
    gains = jnp.concatenate([top, *split(low)], axis=0).astype(bf16)
    gain = dot(jnp.concatenate([hot] * 3, axis=0).astype(bf16), gains, ((0,), (0,)))
    own = (feat_ref[0].astype(f32) * gain).astype(bf16)
    own_ref[...] = own
    gain_out[...] = gain
    ring, core = position()
    for face in range(FACES):
        hot = (rows_iota((ATOMS, GHOST)) == sends_ref[face]).astype(f32)
        picked = dot(hot.astype(bf16), own, ((0,), (0,))).astype(bf16)
        if face < 2:
            pair_ref[lax.rem(core + face, 2)] = picked
        else:
            pick_ref[peer(ring, STRIDES[face - 2])] = picked


def geo_kernel(vec_ref, harm_ref, basis_ref):
    vx, vy, vz = (vec_ref[i] for i in range(3))
    square = vx * vx + vy * vy + vz * vz + 0.25
    inv_r = lax.rsqrt(square)
    radius = square * inv_r
    ux, uy, uz = vx * inv_r, vy * inv_r, vz * inv_r
    r3, r5, r15 = 3.0**0.5, 5.0**0.5, 15.0**0.5
    harms = [
        jnp.ones_like(ux),
        r3 * ux,
        r3 * uy,
        r3 * uz,
        r15 * ux * uy,
        r15 * uy * uz,
        0.5 * r5 * (3.0 * uz * uz - 1.0),
        r15 * ux * uz,
        0.5 * r15 * (ux * ux - uy * uy),
    ]
    for k, h in enumerate(harms):
        harm_ref[k : k + 1, :] = h
    scaled = radius * (1.0 / cutoff)
    envelope = 1.0 - scaled * scaled
    envelope = envelope * envelope * inv_r
    t = scaled * np.float32(np.pi) - np.float32(np.pi / 2)
    t2 = t * t
    sin_t = series(t2, 1) * t
    cos_t = series(t2, 0)
    twice = -2.0 * sin_t
    before, now = jnp.zeros_like(t), cos_t * envelope
    for b in range(NB):
        basis_ref[b : b + 1, :] = now
        before, now = now, twice * now - before


def series(square, odd):
    terms = [(-1.0) ** n / float(np.prod(np.arange(1, 2 * n + odd + 1.0))) for n in range(9)]
    total = jnp.full_like(square, terms[-1])
    for term in terms[-2::-1]:
        total = total * square + term
    return total


def split(values):
    top = values.astype(bf16).astype(f32)
    return top, values - top


def main_kernel(
    own_ref, p0, p1, got_ref, src_ref, dst_ref, harm_ref, basis_ref, wrad_ref, wmix_ref, cot_ref,
    lists_ref, dext_ref, line_ref, send_ref, lists_out,
    hot_s, harm_s, radial_s, source_s, mom_s, dmom_s,
):
    ring, core = position()
    a, b = p0[...].astype(f32), p1[...].astype(f32)
    blocks = [own_ref[...].astype(f32), jnp.where(core == 0, b, a), jnp.where(core == 0, a, b)]
    for stride in STRIDES:
        blocks.append(got_ref[peer(ring, -stride)].astype(f32))
    ext = jnp.concatenate(blocks, axis=0).T.astype(bf16)
    w_top, w_low = split(wrad_ref[...])
    wrad = jnp.concatenate([w_top, w_low, w_top], axis=0).T.astype(bf16)
    turned = jnp.zeros((CHANS, 9 * ATOMS), f32)
    for start in range(0, EDGES, CHUNK):
        at = pl.ds(start, CHUNK)
        src = src_ref[:, at]
        hot = jnp.where(rows_iota((ROWS, CHUNK)) == src, 1.0, 0.0).astype(bf16)
        hot_s[:, at] = hot
        source = dot(ext, hot, ((1,), (0,)))
        source_s[:, at] = source.astype(bf16)
        b_top, b_low = split(basis_ref[:, at])
        basis = jnp.concatenate([b_top, b_top, b_low], axis=0).astype(bf16)
        radial = dot(wrad, basis, ((1,), (0,)))
        radial_s[:, at] = radial
        message = (radial * source).astype(bf16)
        own_hot = rows_iota((ATOMS, CHUNK)) == dst_ref[:, at]
        own_hot = jnp.where(own_hot, 1.0, 0.0).astype(bf16)
        harm_s[0:ATOMS, at] = own_hot
        for k in range(1, 9):
            harm = harm_ref[k : k + 1, at]
            harm_s[k * ATOMS : (k + 1) * ATOMS, at] = own_hot * harm.astype(bf16)
        turned = turned + dot(message, harm_s[:, at], ((1,), (1,)))
    mom_s[...] = turned.T
    moments = [msg_scale * mom_s[k * ATOMS : (k + 1) * ATOMS, :] for k in range(9)]
    squares = [m * m for m in moments]
    two = squares[4]
    for k in range(5, 9):
        two = two + squares[k]
    inv = jnp.concatenate([squares[0], squares[1] + squares[2] + squares[3], two], axis=1).astype(bf16)
    pre = dot(inv, wmix_ref[...], ((1,), (0,)))
    sigma = jax.nn.sigmoid(pre)
    slope = sigma * (1.0 + pre * (1.0 - sigma))
    dpre = (cot_ref[0].astype(f32) * slope).astype(bf16)
    gmix = dot(inv, dpre, ((0,), (0,)))
    nothing = jnp.zeros((GHOST, CHANS), f32)
    for i in range(3 * CHANS // SHARD):
        shard = gmix[i * SHARD : (i + 1) * SHARD]
        send_ref[i] = jnp.concatenate([shard, nothing], axis=0).astype(bf16)
    dinv = dot(dpre, wmix_ref[...], ((1,), (1,)))
    groups = [0, 1, 1, 1, 2, 2, 2, 2, 2]
    for k in range(9):
        part = dinv[:, groups[k] * CHANS : (groups[k] + 1) * CHANS]
        mom_s[k * ATOMS : (k + 1) * ATOMS, :] = (2.0 * msg_scale) * moments[k] * part
    dmom_s[...] = mom_s[...].T.astype(bf16)
    both = jnp.zeros((ROWS + 2 * NB, 2 * CHANS), f32)
    for start in range(0, EDGES, CHUNK):
        at = pl.ds(start, CHUNK)
        dmsg = dot(dmom_s[...], harm_s[:, at], ((1,), (0,)))
        dradial = dmsg * source_s[:, at].astype(f32)
        dsource = (dmsg * radial_s[:, at]).astype(bf16)
        b_top, b_low = split(basis_ref[:, at])
        basis = jnp.concatenate([b_top, b_low], axis=0).astype(bf16)
        left = jnp.concatenate([hot_s[:, at], basis], axis=0)
        right = jnp.concatenate([dsource, dradial.astype(bf16)], axis=0)
        both = both + dot(left, right, ((1,), (1,)))
    dext, gradr = both[:ROWS, :CHANS], both[ROWS:, CHANS:]
    gradr = jnp.concatenate([gradr[:NB] + gradr[NB:], nothing, nothing[:NB]], axis=0)
    send_ref[3 * CHANS // SHARD] = gradr.astype(bf16)
    for i in range(3 * CHANS // SHARD + 1, PEERS):
        send_ref[i] = jnp.zeros((SHARD + GHOST, CHANS), bf16)
    dext_ref[...] = dext[:ATOMS]
    ghosts = [dext[ATOMS + face * GHOST : ATOMS + (face + 1) * GHOST] for face in range(FACES)]
    spot = place()
    for move, block in zip(MOVES, ghosts[:4]):
        to = lax.rem(spot + move + PEERS, PEERS)
        shard = send_ref[to].astype(f32)[:SHARD]
        send_ref[to] = jnp.concatenate([shard, block], axis=0).astype(bf16)
    line_ref[0] = ghosts[4].astype(bf16)
    line_ref[1] = ghosts[5].astype(bf16)
    lists_out[...] = lists_ref[...]


def place():
    return (lax.axis_index("x") * 4 + lax.axis_index("y")) * 2 + lax.axis_index("core")


def passed(got_ref):
    spot = place()
    return [got_ref[lax.rem(spot - move + PEERS, PEERS)].astype(f32)[SHARD:] for move in MOVES]


def add_up(parts_ref, out_ref):
    total = parts_ref[0].astype(f32)[:SHARD]
    for i in range(1, parts_ref.shape[0]):
        total = total + parts_ref[i].astype(f32)[:SHARD]
    total = total.astype(bf16)
    for i in range(out_ref.shape[0]):
        out_ref[i] = total


def slab_kernel(parts_ref, line_ref, out_ref, pass_ref):
    add_up(parts_ref, out_ref)
    blocks = passed(parts_ref)
    odd = lax.rem(lax.axis_index("zl"), 2)
    for i, (down, up) in enumerate([(line_ref[0], line_ref[1]), blocks[:2], blocks[2:]]):
        pass_ref[1 - odd, i] = down.astype(bf16)
        pass_ref[odd, i] = up.astype(bf16)


def line_kernel(parts_ref, out_ref):
    add_up(parts_ref, out_ref)


def post_kernel(
    dext_ref, gain_ref, sends_ref, got_ref, p0, p1, sums_ref, dfeat_ref, gmix_ref, grad_ref
):
    spot = place()
    local = passed(got_ref)
    blocks = []
    a, b = p0[...].astype(f32), p1[...].astype(f32)
    odd = lax.rem(lax.axis_index("zl"), 2)
    down, up = jnp.where(odd == 0, a, b), jnp.where(odd == 0, b, a)
    for move, block, other in zip(MOVES, local, (down[1], up[1], down[2], up[2])):
        crossed = spot - move >= PEERS if move < 0 else spot < move
        blocks.append(jnp.where(crossed, other, block))
    blocks += [down[0], up[0]]
    total = dext_ref[...]
    for face in range(FACES):
        hot = (rows_iota((ATOMS, GHOST)) == sends_ref[face]).astype(f32)
        total = total + dot(hot.astype(bf16), blocks[face].astype(bf16), ((1,), (0,)))
    dfeat_ref[0] = total * gain_ref[...]
    whole = 3 * CHANS // SHARD
    parts = [sums_ref[i].astype(f32) for i in range(whole)]
    grad = sums_ref[whole].astype(f32)[:NB]
    square = grad * grad
    for part in parts:
        for i in range(0, SHARD, NB):
            square = square + part[i : i + NB] * part[i : i + NB]
    norm = jnp.sqrt(jnp.sum(square, keepdims=True))
    factor = clip_norm / jnp.maximum(norm, clip_norm)
    for i, part in enumerate(parts):
        gmix_ref[i * SHARD : (i + 1) * SHARD, :] = factor * part
    grad_ref[...] = factor * grad


def swap(block, parity):
    pairs = []
    for i in range(parity, 128, 2):
        j = (i + 1) % 128
        pairs += [(i, j), (j, i)]
    return lax.ppermute(block, DOM, pairs)


def exchange(blocks, axes):
    return lax.all_to_all(blocks, axes, 0, 0, tiled=True)


def on_device(feat, species, species_gain, send_lists, edge_src, edge_dst, edge_vec, w_rad, w_mix, out_cot):
    shape = jax.ShapeDtypeStruct
    sends = send_lists.reshape(FACES, 1, GHOST)
    own, gain, pair, picks = call(
        pre_kernel,
        [
            shape((ATOMS, CHANS), bf16),
            shape((ATOMS, CHANS), f32),
            shape((2, GHOST, CHANS), bf16),
            shape((RING, GHOST, CHANS), bf16),
        ],
        feat, species, species_gain, sends,
        scratch=[
            pltpu.VMEM((1, ATOMS, CHANS), bf16),
            pltpu.VMEM((1, ATOMS), jnp.int32),
            pltpu.VMEM((5, CHANS), f32),
            pltpu.VMEM((FACES, 1, GHOST), jnp.int32),
            pltpu.SemaphoreType.DMA((4,)),
        ],
        space=pl.ANY,
        limit=60,
    )
    near = [swap(pair[q], q) for q in range(2)]
    far = exchange(picks, PLANE)
    harm, basis = call(
        geo_kernel,
        [shape((16, EDGES), f32), shape((NB, EDGES), f32)],
        edge_vec.reshape(3, 1, EDGES),
        cost=pl.CostEstimate(flops=1000000, bytes_accessed=400000, transcendentals=0),
    )
    dext, line, blocks, lists = call(
        main_kernel,
        [
            shape((ATOMS, CHANS), f32),
            shape((2, GHOST, CHANS), bf16),
            shape((PEERS, SHARD + GHOST, CHANS), bf16),
            shape((FACES, 1, GHOST), jnp.int32),
        ],
        own, *near, far, edge_src, edge_dst, harm, basis, w_rad, w_mix, out_cot, sends,
        scratch=[
            pltpu.VMEM((ROWS, EDGES), bf16),
            pltpu.VMEM((9 * ATOMS, EDGES), bf16),
            pltpu.VMEM((CHANS, EDGES), f32),
            pltpu.VMEM((CHANS, EDGES), bf16),
            pltpu.VMEM((9 * ATOMS, CHANS), f32),
            pltpu.VMEM((CHANS, 9 * ATOMS), bf16),
        ],
    )
    far = exchange(blocks, SLAB)
    parts, passing = call(
        slab_kernel,
        [shape((LINES, SHARD, CHANS), bf16), shape((2, 3, GHOST, CHANS), bf16)],
        far, line,
    )
    pairs = [[(0, 1), (1, 0), (2, 3), (3, 2)], [(1, 2), (2, 1), (3, 0), (0, 3)]]
    passing = [lax.ppermute(passing[q], "zl", pairs[q]) for q in range(2)]
    parts = exchange(parts, LINE)
    (parts,) = call(line_kernel, [shape((PEERS, SHARD, CHANS), bf16)], parts)
    sums = exchange(parts, SLAB)
    d_feat, gmix, grad_r = call(
        post_kernel,
        [shape((1, ATOMS, CHANS), f32), shape((3 * CHANS, CHANS), f32), shape((NB, CHANS), f32)],
        dext, gain, lists, far, *passing, sums,
    )
    return d_feat, gmix, grad_r


def solution(mesh):
    fine = Mesh(mesh.devices.reshape(4, 4, 4, 2, 4), DOM + ("rep",))
    in_specs = (
        P("rep", DOM, None),
        P("rep", DOM),
        P(),
        P("rep", None, DOM),
        P("rep", DOM),
        P("rep", DOM),
        P("rep", None, DOM),
        P(),
        P(),
        P("rep", DOM, None),
    )
    out_specs = (P("rep", DOM, None), P(), P())
    return jax.shard_map(
        on_device, mesh=fine, in_specs=in_specs, out_specs=out_specs, check_vma=False
    )
```

```python
import jax
import jax.numpy as jnp
import numpy as np
from jax import lax
from jax.experimental import pallas as pl
from jax.experimental.pallas import tpu as pltpu
from jax.sharding import Mesh, PartitionSpec as P

msg_scale = 0.35
cutoff = 6.0
clip_norm = 256.0
f32, bf16 = jnp.float32, jnp.bfloat16

CHANS = 128
NB = 8
ATOMS = 64
FACES = 6
GHOST = 24
ROWS = ATOMS + FACES * GHOST
EDGES = 4096
CHUNK = 1024
SHARD = 16
RING = 16
PLANE = ("zl", "x")
PEERS = 32
SLAB = ("x", "y", "core")
LINE = ("zl", "rep")
LINES = 16
MOVES = (-1, 1, -8, 8)
DOM = ("zl", "x", "y", "core")
STRIDES = (1, -1, 4, -4)


def dot(a, b, dims):
    return lax.dot_general(a, b, (dims, ((), ())), preferred_element_type=f32)


def rows_iota(shape):
    return lax.broadcasted_iota(jnp.int32, shape, 0)


def call(kernel, outs, *args, scratch=(), cost=None, space=pltpu.VMEM, limit=48):
    return pl.pallas_call(
        kernel,
        out_shape=outs,
        in_specs=[pl.BlockSpec(memory_space=space) for _ in args],
        out_specs=[pl.BlockSpec(memory_space=pltpu.VMEM) for _ in outs],
        scratch_shapes=list(scratch),
        cost_estimate=cost,
        compiler_params=pltpu.CompilerParams(vmem_limit_bytes=limit * 1024 * 1024),
    )(*args)


def position():
    ring = lax.axis_index("zl") * 4 + lax.axis_index("x")
    return ring, lax.axis_index("core")


def peer(ring, stride):
    return lax.rem(ring + stride + RING, RING)


def pre_kernel(
    feat_hbm, species_hbm, gain_hbm, sends_hbm, own_ref, gain_out, pair_ref, pick_ref,
    feat_ref, species_ref, gain_ref, sends_ref, sems,
):
    copies = [
        pltpu.make_async_copy(src, dst, sems.at[i])
        for i, (src, dst) in enumerate(
            [
                (feat_hbm, feat_ref),
                (species_hbm, species_ref),
                (gain_hbm, gain_ref),
                (sends_hbm, sends_ref),
            ]
        )
    ]
    for copy in copies:
        copy.start()
    pick_ref[...] = jnp.zeros_like(pick_ref)
    for copy in copies:
        copy.wait()
    hot = (rows_iota((8, ATOMS)) == species_ref[...]).astype(f32)
    gains = jnp.concatenate([gain_ref[...], jnp.zeros((3, CHANS), f32)], axis=0)
    top, low = split(gains)
    gains = jnp.concatenate([top, *split(low)], axis=0).astype(bf16)
    gain = dot(jnp.concatenate([hot] * 3, axis=0).astype(bf16), gains, ((0,), (0,)))
    own = (feat_ref[0].astype(f32) * gain).astype(bf16)
    own_ref[...] = own
    gain_out[...] = gain
    ring, core = position()
    for face in range(FACES):
        hot = (rows_iota((ATOMS, GHOST)) == sends_ref[face]).astype(f32)
        picked = dot(hot.astype(bf16), own, ((0,), (0,))).astype(bf16)
        if face < 2:
            pair_ref[lax.rem(core + face, 2)] = picked
        else:
            pick_ref[peer(ring, STRIDES[face - 2])] = picked


def geo_kernel(vec_ref, harm_ref, basis_ref):
    vx, vy, vz = (vec_ref[i] for i in range(3))
    square = vx * vx + vy * vy + vz * vz + 0.25
    inv_r = lax.rsqrt(square)
    radius = square * inv_r
    ux, uy, uz = vx * inv_r, vy * inv_r, vz * inv_r
    r3, r5, r15 = 3.0**0.5, 5.0**0.5, 15.0**0.5
    harms = [
        jnp.ones_like(ux),
        r3 * ux,
        r3 * uy,
        r3 * uz,
        r15 * ux * uy,
        r15 * uy * uz,
        0.5 * r5 * (3.0 * uz * uz - 1.0),
        r15 * ux * uz,
        0.5 * r15 * (ux * ux - uy * uy),
    ]
    for k, h in enumerate(harms):
        harm_ref[k : k + 1, :] = h
    scaled = radius * (1.0 / cutoff)
    envelope = 1.0 - scaled * scaled
    envelope = envelope * envelope * inv_r
    t = scaled * np.float32(np.pi) - np.float32(np.pi / 2)
    t2 = t * t
    sin_t = series(t2, 1) * t
    cos_t = series(t2, 0)
    twice = -2.0 * sin_t
    before, now = jnp.zeros_like(t), cos_t * envelope
    for b in range(NB):
        basis_ref[b : b + 1, :] = now
        before, now = now, twice * now - before


def series(square, odd):
    terms = [(-1.0) ** n / float(np.prod(np.arange(1, 2 * n + odd + 1.0))) for n in range(9)]
    total = jnp.full_like(square, terms[-1])
    for term in terms[-2::-1]:
        total = total * square + term
    return total


def split(values):
    top = values.astype(bf16).astype(f32)
    return top, values - top


def main_kernel(
    own_ref, p0, p1, got_ref, src_ref, dst_ref, harm_ref, basis_ref, wrad_ref, wmix_ref, cot_ref,
    lists_ref, dext_ref, local_ref, pass_ref, send_ref, lists_out,
    hot_s, harm_s, radial_s, source_s, mom_s, dmom_s,
):
    ring, core = position()
    a, b = p0[...].astype(f32), p1[...].astype(f32)
    blocks = [own_ref[...].astype(f32), jnp.where(core == 0, b, a), jnp.where(core == 0, a, b)]
    for stride in STRIDES:
        blocks.append(got_ref[peer(ring, -stride)].astype(f32))
    ext = jnp.concatenate(blocks, axis=0).T.astype(bf16)
    w_top, w_low = split(wrad_ref[...])
    wrad = jnp.concatenate([w_top, w_low, w_top], axis=0).T.astype(bf16)
    turned = jnp.zeros((CHANS, 9 * ATOMS), f32)
    for start in range(0, EDGES, CHUNK):
        at = pl.ds(start, CHUNK)
        src = src_ref[:, at]
        hot = jnp.where(rows_iota((ROWS, CHUNK)) == src, 1.0, 0.0).astype(bf16)
        hot_s[:, at] = hot
        source = dot(ext, hot, ((1,), (0,)))
        source_s[:, at] = source.astype(bf16)
        b_top, b_low = split(basis_ref[:, at])
        basis = jnp.concatenate([b_top, b_top, b_low], axis=0).astype(bf16)
        radial = dot(wrad, basis, ((1,), (0,)))
        radial_s[:, at] = radial
        message = (radial * source).astype(bf16)
        own_hot = rows_iota((ATOMS, CHUNK)) == dst_ref[:, at]
        own_hot = jnp.where(own_hot, 1.0, 0.0).astype(bf16)
        harm_s[0:ATOMS, at] = own_hot
        for k in range(1, 9):
            harm = harm_ref[k : k + 1, at]
            harm_s[k * ATOMS : (k + 1) * ATOMS, at] = own_hot * harm.astype(bf16)
        turned = turned + dot(message, harm_s[:, at], ((1,), (1,)))
    mom_s[...] = turned.T
    moments = [msg_scale * mom_s[k * ATOMS : (k + 1) * ATOMS, :] for k in range(9)]
    squares = [m * m for m in moments]
    two = squares[4]
    for k in range(5, 9):
        two = two + squares[k]
    inv = jnp.concatenate([squares[0], squares[1] + squares[2] + squares[3], two], axis=1).astype(bf16)
    pre = dot(inv, wmix_ref[...], ((1,), (0,)))
    sigma = jax.nn.sigmoid(pre)
    slope = sigma * (1.0 + pre * (1.0 - sigma))
    dpre = (cot_ref[0].astype(f32) * slope).astype(bf16)
    gmix = dot(inv, dpre, ((0,), (0,)))
    nothing = jnp.zeros((GHOST, CHANS), f32)
    for i in range(3 * CHANS // SHARD):
        shard = gmix[i * SHARD : (i + 1) * SHARD]
        send_ref[i] = shard.astype(bf16)
    dinv = dot(dpre, wmix_ref[...], ((1,), (1,)))
    groups = [0, 1, 1, 1, 2, 2, 2, 2, 2]
    for k in range(9):
        part = dinv[:, groups[k] * CHANS : (groups[k] + 1) * CHANS]
        mom_s[k * ATOMS : (k + 1) * ATOMS, :] = (2.0 * msg_scale) * moments[k] * part
    dmom_s[...] = mom_s[...].T.astype(bf16)
    both = jnp.zeros((ROWS + 2 * NB, 2 * CHANS), f32)
    for start in range(0, EDGES, CHUNK):
        at = pl.ds(start, CHUNK)
        dmsg = dot(dmom_s[...], harm_s[:, at], ((1,), (0,)))
        dradial = dmsg * source_s[:, at].astype(f32)
        dsource = (dmsg * radial_s[:, at]).astype(bf16)
        b_top, b_low = split(basis_ref[:, at])
        basis = jnp.concatenate([b_top, b_low], axis=0).astype(bf16)
        left = jnp.concatenate([hot_s[:, at], basis], axis=0)
        right = jnp.concatenate([dsource, dradial.astype(bf16)], axis=0)
        both = both + dot(left, right, ((1,), (1,)))
    dext, gradr = both[:ROWS, :CHANS], both[ROWS:, CHANS:]
    gradr = jnp.concatenate([gradr[:NB] + gradr[NB:], nothing[: SHARD - NB]], axis=0)
    send_ref[3 * CHANS // SHARD] = gradr.astype(bf16)
    for i in range(3 * CHANS // SHARD + 1, PEERS):
        send_ref[i] = jnp.zeros((SHARD, CHANS), bf16)
    dext_ref[...] = dext[:ATOMS]
    ghosts = [dext[ATOMS + face * GHOST : ATOMS + (face + 1) * GHOST] for face in range(FACES)]
    ghosts = [block.astype(bf16) for block in ghosts]
    odd = lax.rem(lax.axis_index("zl"), 2)
    for i in range(4):
        local_ref[i] = ghosts[i]
    for i, pair in enumerate((4, 0, 2)):
        pass_ref[1 - odd, i] = ghosts[pair]
        pass_ref[odd, i] = ghosts[pair + 1]
    lists_out[...] = lists_ref[...]


def place():
    return (lax.axis_index("x") * 4 + lax.axis_index("y")) * 2 + lax.axis_index("core")


def total_of(parts_ref):
    total = parts_ref[0].astype(f32)
    for i in range(1, parts_ref.shape[0]):
        total = total + parts_ref[i].astype(f32)
    return total


def crossed(p0, p1):
    odd = lax.rem(lax.axis_index("zl"), 2)
    a, b = p0[...].astype(f32), p1[...].astype(f32)
    return jnp.where(odd == 0, a, b), jnp.where(odd == 0, b, a)


def slab_kernel(parts_ref, p0, p1, out_ref):
    total = total_of(parts_ref).astype(bf16)
    for i in range(LINES):
        out_ref[i] = total


def line_kernel(parts_ref, local_ref, p0, p1, out_ref):
    total = total_of(parts_ref)
    plain = jnp.concatenate([total, jnp.zeros((GHOST, CHANS), f32)], axis=0).astype(bf16)
    for i in range(PEERS):
        out_ref[i] = plain
    down, up = crossed(p0, p1)
    spot = place()
    for i, (move, other) in enumerate(zip(MOVES, (down[1], up[1], down[2], up[2]))):
        leaves = spot < -move if move < 0 else spot + move >= PEERS
        block = jnp.where(leaves, other, local_ref[i].astype(f32))
        block = jnp.concatenate([total, block], axis=0).astype(bf16)
        out_ref[lax.rem(spot + move + PEERS, PEERS)] = block


def post_kernel(
    dext_ref, gain_ref, sends_ref, p0, p1, sums_ref, dfeat_ref, gmix_ref, grad_ref
):
    spot = place()
    down, up = crossed(p0, p1)
    blocks = [
        sums_ref[lax.rem(spot - move + PEERS, PEERS)].astype(f32)[SHARD:] for move in MOVES
    ]
    blocks += [down[0], up[0]]
    total = dext_ref[...]
    for face in range(FACES):
        hot = (rows_iota((ATOMS, GHOST)) == sends_ref[face]).astype(f32)
        total = total + dot(hot.astype(bf16), blocks[face].astype(bf16), ((1,), (0,)))
    dfeat_ref[0] = total * gain_ref[...]
    whole = 3 * CHANS // SHARD
    parts = [sums_ref[i].astype(f32)[:SHARD] for i in range(whole)]
    grad = sums_ref[whole].astype(f32)[:NB]
    square = grad * grad
    for part in parts:
        for i in range(0, SHARD, NB):
            square = square + part[i : i + NB] * part[i : i + NB]
    norm = jnp.sqrt(jnp.sum(square, keepdims=True))
    factor = clip_norm / jnp.maximum(norm, clip_norm)
    for i, part in enumerate(parts):
        gmix_ref[i * SHARD : (i + 1) * SHARD, :] = factor * part
    grad_ref[...] = factor * grad


def swap(block, parity):
    pairs = []
    for i in range(parity, 128, 2):
        j = (i + 1) % 128
        pairs += [(i, j), (j, i)]
    return lax.ppermute(block, DOM, pairs)


def exchange(blocks, axes):
    return lax.all_to_all(blocks, axes, 0, 0, tiled=True)


def on_device(feat, species, species_gain, send_lists, edge_src, edge_dst, edge_vec, w_rad, w_mix, out_cot):
    shape = jax.ShapeDtypeStruct
    sends = send_lists.reshape(FACES, 1, GHOST)
    own, gain, pair, picks = call(
        pre_kernel,
        [
            shape((ATOMS, CHANS), bf16),
            shape((ATOMS, CHANS), f32),
            shape((2, GHOST, CHANS), bf16),
            shape((RING, GHOST, CHANS), bf16),
        ],
        feat, species, species_gain, sends,
        scratch=[
            pltpu.VMEM((1, ATOMS, CHANS), bf16),
            pltpu.VMEM((1, ATOMS), jnp.int32),
            pltpu.VMEM((5, CHANS), f32),
            pltpu.VMEM((FACES, 1, GHOST), jnp.int32),
            pltpu.SemaphoreType.DMA((4,)),
        ],
        space=pl.ANY,
        limit=60,
    )
    near = [swap(pair[q], q) for q in range(2)]
    far = exchange(picks, PLANE)
    harm, basis = call(
        geo_kernel,
        [shape((16, EDGES), f32), shape((NB, EDGES), f32)],
        edge_vec.reshape(3, 1, EDGES),
        cost=pl.CostEstimate(flops=1000000, bytes_accessed=400000, transcendentals=0),
    )
    dext, local, passing, parts, lists = call(
        main_kernel,
        [
            shape((ATOMS, CHANS), f32),
            shape((4, GHOST, CHANS), bf16),
            shape((2, 3, GHOST, CHANS), bf16),
            shape((PEERS, SHARD, CHANS), bf16),
            shape((FACES, 1, GHOST), jnp.int32),
        ],
        own, *near, far, edge_src, edge_dst, harm, basis, w_rad, w_mix, out_cot, sends,
        scratch=[
            pltpu.VMEM((ROWS, EDGES), bf16),
            pltpu.VMEM((9 * ATOMS, EDGES), bf16),
            pltpu.VMEM((CHANS, EDGES), f32),
            pltpu.VMEM((CHANS, EDGES), bf16),
            pltpu.VMEM((9 * ATOMS, CHANS), f32),
            pltpu.VMEM((CHANS, 9 * ATOMS), bf16),
        ],
    )
    pairs = [[(0, 1), (1, 0), (2, 3), (3, 2)], [(1, 2), (2, 1), (3, 0), (0, 3)]]
    passing = [lax.ppermute(passing[q], "zl", pairs[q]) for q in range(2)]
    parts = exchange(parts, SLAB)
    (parts,) = call(slab_kernel, [shape((LINES, SHARD, CHANS), bf16)], parts, *passing)
    parts = exchange(parts, LINE)
    (parts,) = call(
        line_kernel, [shape((PEERS, SHARD + GHOST, CHANS), bf16)], parts, local, *passing
    )
    sums = exchange(parts, SLAB)
    d_feat, gmix, grad_r = call(
        post_kernel,
        [shape((1, ATOMS, CHANS), f32), shape((3 * CHANS, CHANS), f32), shape((NB, CHANS), f32)],
        dext, gain, lists, *passing, sums,
    )
    return d_feat, gmix, grad_r


def solution(mesh):
    fine = Mesh(mesh.devices.reshape(4, 4, 4, 2, 4), DOM + ("rep",))
    in_specs = (
        P("rep", DOM, None),
        P("rep", DOM),
        P(),
        P("rep", None, DOM),
        P("rep", DOM),
        P("rep", DOM),
        P("rep", None, DOM),
        P(),
        P(),
        P("rep", DOM, None),
    )
    out_specs = (P("rep", DOM, None), P(), P())
    return jax.shard_map(
        on_device, mesh=fine, in_specs=in_specs, out_specs=out_specs, check_vma=False
    )
```

```python
import jax
import jax.numpy as jnp
import numpy as np
from jax import lax
from jax.experimental import pallas as pl
from jax.experimental.pallas import tpu as pltpu
from jax.sharding import Mesh, PartitionSpec as P

msg_scale = 0.35
cutoff = 6.0
clip_norm = 256.0
f32, bf16 = jnp.float32, jnp.bfloat16

CHANS = 128
NB = 8
ATOMS = 64
FACES = 6
GHOST = 24
ROWS = ATOMS + FACES * GHOST
EDGES = 4096
CHUNK = 1024
SHARD = 16
RING = 16
PLANE = ("zl", "x")
PEERS = 32
SLAB = ("x", "y", "core")
LINE = ("zl", "rep")
LINES = 16
MOVES = (-1, 1, -8, 8)
DOM = ("zl", "x", "y", "core")
STRIDES = (1, -1, 4, -4)


def dot(a, b, dims):
    return lax.dot_general(a, b, (dims, ((), ())), preferred_element_type=f32)


def rows_iota(shape):
    return lax.broadcasted_iota(jnp.int32, shape, 0)


def call(kernel, outs, *args, scratch=(), cost=None, space=pltpu.VMEM, limit=48):
    return pl.pallas_call(
        kernel,
        out_shape=outs,
        in_specs=[pl.BlockSpec(memory_space=space) for _ in args],
        out_specs=[pl.BlockSpec(memory_space=pltpu.VMEM) for _ in outs],
        scratch_shapes=list(scratch),
        cost_estimate=cost,
        compiler_params=pltpu.CompilerParams(vmem_limit_bytes=limit * 1024 * 1024),
    )(*args)


def position():
    ring = lax.axis_index("zl") * 4 + lax.axis_index("x")
    return ring, lax.axis_index("core")


def peer(ring, stride):
    return lax.rem(ring + stride + RING, RING)


def pre_kernel(
    feat_hbm, species_hbm, gain_hbm, sends_hbm, own_ref, gain_out, first_ref, second_ref, pick_ref,
    feat_ref, species_ref, gain_ref, sends_ref, sems,
):
    copies = [
        pltpu.make_async_copy(src, dst, sems.at[i])
        for i, (src, dst) in enumerate(
            [
                (feat_hbm, feat_ref),
                (species_hbm, species_ref),
                (gain_hbm, gain_ref),
                (sends_hbm, sends_ref),
            ]
        )
    ]
    for copy in copies:
        copy.start()
    pick_ref[...] = jnp.zeros_like(pick_ref)
    for copy in copies:
        copy.wait()
    hot = (rows_iota((8, ATOMS)) == species_ref[...]).astype(f32)
    gains = jnp.concatenate([gain_ref[...], jnp.zeros((3, CHANS), f32)], axis=0)
    top, low = split(gains)
    gains = jnp.concatenate([top, *split(low)], axis=0).astype(bf16)
    gain = dot(jnp.concatenate([hot] * 3, axis=0).astype(bf16), gains, ((0,), (0,)))
    own = (feat_ref[0].astype(f32) * gain).astype(bf16)
    own_ref[...] = own
    gain_out[...] = gain
    ring, core = position()
    near = []
    for face in range(FACES):
        hot = (rows_iota((ATOMS, GHOST)) == sends_ref[face]).astype(f32)
        picked = dot(hot.astype(bf16), own, ((0,), (0,)))
        if face < 2:
            near.append(picked)
        else:
            pick_ref[peer(ring, STRIDES[face - 2])] = picked.astype(bf16)
    first_ref[...] = jnp.where(core == 0, near[0], near[1]).astype(bf16)
    second_ref[...] = jnp.where(core == 0, near[1], near[0]).astype(bf16)


def geo_kernel(vec_ref, harm_ref, basis_ref):
    vx, vy, vz = (vec_ref[i] for i in range(3))
    square = vx * vx + vy * vy + vz * vz + 0.25
    inv_r = lax.rsqrt(square)
    radius = square * inv_r
    ux, uy, uz = vx * inv_r, vy * inv_r, vz * inv_r
    r3, r5, r15 = 3.0**0.5, 5.0**0.5, 15.0**0.5
    harms = [
        jnp.ones_like(ux),
        r3 * ux,
        r3 * uy,
        r3 * uz,
        r15 * ux * uy,
        r15 * uy * uz,
        0.5 * r5 * (3.0 * uz * uz - 1.0),
        r15 * ux * uz,
        0.5 * r15 * (ux * ux - uy * uy),
    ]
    for k, h in enumerate(harms):
        harm_ref[k : k + 1, :] = h
    scaled = radius * (1.0 / cutoff)
    envelope = 1.0 - scaled * scaled
    envelope = envelope * envelope * inv_r
    t = scaled * np.float32(np.pi) - np.float32(np.pi / 2)
    t2 = t * t
    sin_t = series(t2, 1) * t
    cos_t = series(t2, 0)
    twice = -2.0 * sin_t
    before, now = jnp.zeros_like(t), cos_t * envelope
    for b in range(NB):
        basis_ref[b : b + 1, :] = now
        before, now = now, twice * now - before


def series(square, odd):
    terms = [(-1.0) ** n / float(np.prod(np.arange(1, 2 * n + odd + 1.0))) for n in range(9)]
    total = jnp.full_like(square, terms[-1])
    for term in terms[-2::-1]:
        total = total * square + term
    return total


def split(values):
    top = values.astype(bf16).astype(f32)
    return top, values - top


def main_kernel(
    own_ref, p0, p1, got_ref, src_ref, dst_ref, harm_ref, basis_ref, wrad_ref, wmix_ref, cot_ref,
    lists_ref, dext_ref, line_ref, send_ref, lists_out,
    hot_s, harm_s, radial_s, source_s, mom_s, dmom_s,
):
    ring, core = position()
    a, b = p0[...].astype(f32), p1[...].astype(f32)
    blocks = [own_ref[...].astype(f32), jnp.where(core == 0, b, a), jnp.where(core == 0, a, b)]
    for stride in STRIDES:
        blocks.append(got_ref[peer(ring, -stride)].astype(f32))
    ext = jnp.concatenate(blocks, axis=0).T.astype(bf16)
    w_top, w_low = split(wrad_ref[...])
    wrad = jnp.concatenate([w_top, w_low, w_top], axis=0).T.astype(bf16)
    turned = jnp.zeros((CHANS, 9 * ATOMS), f32)
    for start in range(0, EDGES, CHUNK):
        at = pl.ds(start, CHUNK)
        src = src_ref[:, at]
        hot = jnp.where(rows_iota((ROWS, CHUNK)) == src, 1.0, 0.0).astype(bf16)
        hot_s[:, at] = hot
        source = dot(ext, hot, ((1,), (0,)))
        source_s[:, at] = source.astype(bf16)
        b_top, b_low = split(basis_ref[:, at])
        basis = jnp.concatenate([b_top, b_top, b_low], axis=0).astype(bf16)
        radial = dot(wrad, basis, ((1,), (0,)))
        radial_s[:, at] = radial
        message = (radial * source).astype(bf16)
        own_hot = rows_iota((ATOMS, CHUNK)) == dst_ref[:, at]
        own_hot = jnp.where(own_hot, 1.0, 0.0).astype(bf16)
        harm_s[0:ATOMS, at] = own_hot
        for k in range(1, 9):
            harm = harm_ref[k : k + 1, at]
            harm_s[k * ATOMS : (k + 1) * ATOMS, at] = own_hot * harm.astype(bf16)
        turned = turned + dot(message, harm_s[:, at], ((1,), (1,)))
    mom_s[...] = turned.T
    moments = [msg_scale * mom_s[k * ATOMS : (k + 1) * ATOMS, :] for k in range(9)]
    squares = [m * m for m in moments]
    two = squares[4]
    for k in range(5, 9):
        two = two + squares[k]
    inv = jnp.concatenate([squares[0], squares[1] + squares[2] + squares[3], two], axis=1).astype(bf16)
    pre = dot(inv, wmix_ref[...], ((1,), (0,)))
    sigma = jax.nn.sigmoid(pre)
    slope = sigma * (1.0 + pre * (1.0 - sigma))
    dpre = (cot_ref[0].astype(f32) * slope).astype(bf16)
    gmix = dot(inv, dpre, ((0,), (0,)))
    nothing = jnp.zeros((GHOST, CHANS), f32)
    for i in range(3 * CHANS // SHARD):
        shard = gmix[i * SHARD : (i + 1) * SHARD]
        send_ref[i] = jnp.concatenate([shard, nothing], axis=0).astype(bf16)
    dinv = dot(dpre, wmix_ref[...], ((1,), (1,)))
    groups = [0, 1, 1, 1, 2, 2, 2, 2, 2]
    for k in range(9):
        part = dinv[:, groups[k] * CHANS : (groups[k] + 1) * CHANS]
        mom_s[k * ATOMS : (k + 1) * ATOMS, :] = (2.0 * msg_scale) * moments[k] * part
    dmom_s[...] = mom_s[...].T.astype(bf16)
    both = jnp.zeros((ROWS + 2 * NB, 2 * CHANS), f32)
    for start in range(0, EDGES, CHUNK):
        at = pl.ds(start, CHUNK)
        dmsg = dot(dmom_s[...], harm_s[:, at], ((1,), (0,)))
        dradial = dmsg * source_s[:, at].astype(f32)
        dsource = (dmsg * radial_s[:, at]).astype(bf16)
        b_top, b_low = split(basis_ref[:, at])
        basis = jnp.concatenate([b_top, b_low], axis=0).astype(bf16)
        left = jnp.concatenate([hot_s[:, at], basis], axis=0)
        right = jnp.concatenate([dsource, dradial.astype(bf16)], axis=0)
        both = both + dot(left, right, ((1,), (1,)))
    dext, gradr = both[:ROWS, :CHANS], both[ROWS:, CHANS:]
    gradr = jnp.concatenate([gradr[:NB] + gradr[NB:], nothing, nothing[:NB]], axis=0)
    send_ref[3 * CHANS // SHARD] = gradr.astype(bf16)
    for i in range(3 * CHANS // SHARD + 1, PEERS):
        send_ref[i] = jnp.zeros((SHARD + GHOST, CHANS), bf16)
    dext_ref[...] = dext[:ATOMS]
    ghosts = [dext[ATOMS + face * GHOST : ATOMS + (face + 1) * GHOST] for face in range(FACES)]
    spot = place()
    for move, block in zip(MOVES, ghosts[:4]):
        to = lax.rem(spot + move + PEERS, PEERS)
        shard = send_ref[to].astype(f32)[:SHARD]
        send_ref[to] = jnp.concatenate([shard, block], axis=0).astype(bf16)
    line_ref[0] = ghosts[4].astype(bf16)
    line_ref[1] = ghosts[5].astype(bf16)
    lists_out[...] = lists_ref[...]


def place():
    return (lax.axis_index("x") * 4 + lax.axis_index("y")) * 2 + lax.axis_index("core")


def passed(got_ref):
    spot = place()
    return [got_ref[lax.rem(spot - move + PEERS, PEERS)].astype(f32)[SHARD:] for move in MOVES]


def add_up(parts_ref, out_ref):
    total = parts_ref[0].astype(f32)[:SHARD]
    for i in range(1, parts_ref.shape[0]):
        total = total + parts_ref[i].astype(f32)[:SHARD]
    total = total.astype(bf16)
    for i in range(out_ref.shape[0]):
        out_ref[i] = total


def slab_kernel(parts_ref, line_ref, out_ref, pass_ref):
    add_up(parts_ref, out_ref)
    blocks = passed(parts_ref)
    odd = lax.rem(lax.axis_index("zl"), 2)
    for i, (down, up) in enumerate([(line_ref[0], line_ref[1]), blocks[:2], blocks[2:]]):
        pass_ref[1 - odd, i] = down.astype(bf16)
        pass_ref[odd, i] = up.astype(bf16)


def line_kernel(parts_ref, p0, p1, out_ref):
    add_up(parts_ref, out_ref)


def post_kernel(
    dext_ref, gain_ref, sends_ref, got_ref, p0, p1, sums_ref, dfeat_ref, gmix_ref, grad_ref
):
    spot = place()
    local = passed(got_ref)
    blocks = []
    a, b = p0[...].astype(f32), p1[...].astype(f32)
    odd = lax.rem(lax.axis_index("zl"), 2)
    down, up = jnp.where(odd == 0, a, b), jnp.where(odd == 0, b, a)
    for move, block, other in zip(MOVES, local, (down[1], up[1], down[2], up[2])):
        crossed = spot - move >= PEERS if move < 0 else spot < move
        blocks.append(jnp.where(crossed, other, block))
    blocks += [down[0], up[0]]
    total = dext_ref[...]
    for face in range(FACES):
        hot = (rows_iota((ATOMS, GHOST)) == sends_ref[face]).astype(f32)
        total = total + dot(hot.astype(bf16), blocks[face].astype(bf16), ((1,), (0,)))
    dfeat_ref[0] = total * gain_ref[...]
    whole = 3 * CHANS // SHARD
    parts = [sums_ref[i].astype(f32) for i in range(whole)]
    grad = sums_ref[whole].astype(f32)[:NB]
    square = grad * grad
    for part in parts:
        for i in range(0, SHARD, NB):
            square = square + part[i : i + NB] * part[i : i + NB]
    norm = jnp.sqrt(jnp.sum(square, keepdims=True))
    factor = clip_norm / jnp.maximum(norm, clip_norm)
    for i, part in enumerate(parts):
        gmix_ref[i * SHARD : (i + 1) * SHARD, :] = factor * part
    grad_ref[...] = factor * grad


def swap(block, parity):
    pairs = []
    for i in range(parity, 128, 2):
        j = (i + 1) % 128
        pairs += [(i, j), (j, i)]
    return lax.ppermute(block, DOM, pairs)


def exchange(blocks, axes):
    return lax.all_to_all(blocks, axes, 0, 0, tiled=True)


def on_device(feat, species, species_gain, send_lists, edge_src, edge_dst, edge_vec, w_rad, w_mix, out_cot):
    shape = jax.ShapeDtypeStruct
    sends = send_lists.reshape(FACES, 1, GHOST)
    own, gain, first, second, picks = call(
        pre_kernel,
        [
            shape((ATOMS, CHANS), bf16),
            shape((ATOMS, CHANS), f32),
            shape((GHOST, CHANS), bf16),
            shape((GHOST, CHANS), bf16),
            shape((RING, GHOST, CHANS), bf16),
        ],
        feat, species, species_gain, sends,
        scratch=[
            pltpu.VMEM((1, ATOMS, CHANS), bf16),
            pltpu.VMEM((1, ATOMS), jnp.int32),
            pltpu.VMEM((5, CHANS), f32),
            pltpu.VMEM((FACES, 1, GHOST), jnp.int32),
            pltpu.SemaphoreType.DMA((4,)),
        ],
        space=pl.ANY,
        limit=60,
    )
    near = [swap(first, 0), swap(second, 1)]
    far = exchange(picks, PLANE)
    harm, basis = call(
        geo_kernel,
        [shape((16, EDGES), f32), shape((NB, EDGES), f32)],
        edge_vec.reshape(3, 1, EDGES),
        cost=pl.CostEstimate(flops=1000000, bytes_accessed=400000, transcendentals=0),
    )
    dext, line, blocks, lists = call(
        main_kernel,
        [
            shape((ATOMS, CHANS), f32),
            shape((2, GHOST, CHANS), bf16),
            shape((PEERS, SHARD + GHOST, CHANS), bf16),
            shape((FACES, 1, GHOST), jnp.int32),
        ],
        own, *near, far, edge_src, edge_dst, harm, basis, w_rad, w_mix, out_cot, sends,
        scratch=[
            pltpu.VMEM((ROWS, EDGES), bf16),
            pltpu.VMEM((9 * ATOMS, EDGES), bf16),
            pltpu.VMEM((CHANS, EDGES), f32),
            pltpu.VMEM((CHANS, EDGES), bf16),
            pltpu.VMEM((9 * ATOMS, CHANS), f32),
            pltpu.VMEM((CHANS, 9 * ATOMS), bf16),
        ],
    )
    far = exchange(blocks, SLAB)
    parts, passing = call(
        slab_kernel,
        [shape((LINES, SHARD, CHANS), bf16), shape((2, 3, GHOST, CHANS), bf16)],
        far, line,
    )
    pairs = [[(0, 1), (1, 0), (2, 3), (3, 2)], [(1, 2), (2, 1), (3, 0), (0, 3)]]
    passing = [lax.ppermute(passing[q], "zl", pairs[q]) for q in range(2)]
    parts = exchange(parts, LINE)
    (parts,) = call(line_kernel, [shape((PEERS, SHARD, CHANS), bf16)], parts, *passing)
    sums = exchange(parts, SLAB)
    d_feat, gmix, grad_r = call(
        post_kernel,
        [shape((1, ATOMS, CHANS), f32), shape((3 * CHANS, CHANS), f32), shape((NB, CHANS), f32)],
        dext, gain, lists, far, *passing, sums,
    )
    return d_feat, gmix, grad_r


def solution(mesh):
    fine = Mesh(mesh.devices.reshape(4, 4, 4, 2, 4), DOM + ("rep",))
    in_specs = (
        P("rep", DOM, None),
        P("rep", DOM),
        P(),
        P("rep", None, DOM),
        P("rep", DOM),
        P("rep", DOM),
        P("rep", None, DOM),
        P(),
        P(),
        P("rep", DOM, None),
    )
    out_specs = (P("rep", DOM, None), P(), P())
    return jax.shard_map(
        on_device, mesh=fine, in_specs=in_specs, out_specs=out_specs, check_vma=False
    )
```
